1024 devices in a mesh: ctx: 64 (over y, x), head: 16 (over z, core).
Axes of the slice: x: 8, y: 8, z: 8, core: 2. Of those that a mesh axis runs over, the one named last changes fastest.
Arguments:
- queries: bfloat16 [8192, 8192], P('ctx', 'head'), may hold values from -6 to 6
- key_rows: bfloat16 [8192, 8192], P('ctx', 'head'), may hold values from -6 to 6
- value_rows: bfloat16 [8192, 8192], P('ctx', 'head'), may hold values from -6 to 6
- gate_in: bfloat16 [8192, 8192], P('ctx', 'head'), may hold values from -6 to 6
- grad_out: bfloat16 [8192, 8192], P('ctx', 'head'), may hold values from -6 to 6
- decay_ints: int32 [64], P('head'), may hold values from 1 to 32767, as said below
- norm_gain: float32 [8192], P('head'), may hold values from 0.1 to 1.9
Outputs:
- grad_queries: bfloat16 [8192, 8192], P('ctx', 'head')
- grad_keys: bfloat16 [8192, 8192], P('ctx', 'head')
- grad_values: bfloat16 [8192, 8192], P('ctx', 'head')
- grad_gate: bfloat16 [8192, 8192], P('ctx', 'head')
- grad_gain: float32 [8192], P('head')
The draws below stay inside these ranges and needn't reach their ends.
Inputs may be any that keep to these rules, and one draw needn't show every extreme that they name: Head h forgets as exp(-decay_ints[h] / 1048576) per token.
All inputs are finite; a program needn't handle non-finite values.
Results may differ from the reference program's by a relative error of at most 0.005.
Values sent between devices are 32-bit elements; how exact they have to be, the bound alone decides.
No kernel may reach another device: no remote copies, remote signals or barrier semaphores. Data moves between devices by JAX's collectives and lax.ppermute only.
A program may use at most 128 MiB of HBM per device.

```python
import jax
import jax.numpy as jnp
from jax import lax

H = 64
DH = 128
TOK_DEV = 128
TOKENS = 8192
HD = 8192
N_CTX = 64


def draw_decay_ints(key, part):
    key = jax.random.fold_in(key, 11)
    first, second = jax.random.split(key)
    octave = jax.random.randint(first, (H,), 0, 15)
    base = jnp.left_shift(jnp.ones((H,), jnp.int32), octave)
    extra = jnp.bitwise_and(jax.random.randint(second, (H,), 0, 32768), base - 1)
    return (base + extra).astype(jnp.int32)


def levels(rng, shape, cuts, smallest, largest):
    gain, own = 1.0, jax.random.fold_in(rng, 6)
    for axis_at, blocks in cuts:
        draws = jnp.exp(jax.random.uniform(jax.random.fold_in(own, axis_at), (blocks,), jnp.float32, smallest / len(cuts), largest / len(cuts)))
        gain = gain * jnp.repeat(draws, shape[axis_at] // blocks).reshape([-1 if axis == axis_at else 1 for axis in range(len(shape))])
    return gain


def centred(key, dims, scale, most, pieces=(), held_as=jnp.bfloat16):
    level = levels(key, dims, pieces, -0.22, 0.18) if pieces else 1.0
    result = jax.random.normal(key, dims, jnp.float32) * scale * level
    return jnp.minimum(jnp.maximum(result, -most), most).astype(held_as)


def setup_inputs(seed: int = 0) -> dict:
    seeds = jax.random.split(jax.random.key(seed), 8)
    return {
        "queries": centred(seeds[0], (TOKENS, HD), 1.0, 6.0, ((0, 64), (1, 16))),
        "key_rows": centred(seeds[1], (TOKENS, HD), 1.0, 6.0, ((0, 64), (1, 16))),
        "value_rows": centred(seeds[2], (TOKENS, HD), 1.0, 6.0, ((0, 64), (1, 16))),
        "gate_in": centred(seeds[3], (TOKENS, HD), 1.5, 6.0, ((0, 64), (1, 16))),
        "grad_out": centred(seeds[4], (TOKENS, HD), 1.0, 6.0, ((0, 64), (1, 16))),
        "decay_ints": draw_decay_ints(jax.random.fold_in(seeds[7], 71), 0),
        "norm_gain": jnp.clip(1.0 + 0.18 * jax.random.normal(seeds[6], (HD,), jnp.float32), 0.1, 1.9),
    }


rate_unit = 2.0 ** (-20)
norm_eps = 1e-06

def decay_tables(decay_rate):
    positions = jnp.arange(TOK_DEV, dtype=jnp.float32)
    early_decay = jnp.exp(-decay_rate[None, :] * (positions[:, None] + 1.0))
    late_decay = jnp.exp(-decay_rate[None, :] * (TOK_DEV - 1.0 - positions[:, None]))
    distance = positions[:, None] - positions[None, :]
    decay_matrix = jnp.where(distance[None] >= 0.0, jnp.exp(-decay_rate[:, None, None] * jnp.maximum(distance, 0.0)[None]), 0.0) / DH
    block_span = jnp.exp(-decay_rate * TOK_DEV)
    return (early_decay, late_decay, decay_matrix, block_span)

def forward_block(query_blk, key_blk, value_blk, prefix, early_decay, decay_matrix):
    scores = jnp.einsum('thd,shd->hts', query_blk.astype(jnp.float32), key_blk.astype(jnp.float32))
    attn_weights = (scores * decay_matrix).astype(jnp.bfloat16)
    output = jnp.einsum('hts,she->the', attn_weights.astype(jnp.float32), value_blk.astype(jnp.float32))
    carried = jnp.einsum('thd,hde->the', query_blk.astype(jnp.float32), prefix, precision=lax.Precision.HIGHEST)
    return (output + early_decay[:, :, None] * carried / DH, attn_weights)

def reference(queries, key_rows, value_rows, gate_in, grad_out, decay_ints, norm_gain):
    decay_rate = decay_ints.astype(jnp.float32) * rate_unit
    early_decay, late_decay, decay_matrix, block_span = decay_tables(decay_rate)
    query_blocks = queries.reshape(N_CTX, TOK_DEV, H, DH)
    key_blocks = key_rows.reshape(N_CTX, TOK_DEV, H, DH)
    value_blocks = value_rows.reshape(N_CTX, TOK_DEV, H, DH)
    gate_blocks = gate_in.reshape(N_CTX, TOK_DEV, H * DH)
    cot_blocks = grad_out.reshape(N_CTX, TOK_DEV, H * DH)

    def summarize(pair):
        weighted = late_decay[:, :, None] * pair[0].astype(jnp.float32)
        return jnp.einsum('shd,she->hde', weighted, pair[1].astype(jnp.float32), precision=lax.Precision.HIGHEST)
    summaries = lax.map(summarize, (key_blocks, value_blocks))

    def step_state(carry, summ):
        return (block_span[:, None, None] * carry + summ, carry)
    _, prefixes = lax.scan(step_state, jnp.zeros((H, DH, DH), jnp.float32), summaries)

    def norm_block(items):
        query_blk, key_blk, value_blk, gate_blk, cot_blk, prefix = items
        attention, attn_weights = forward_block(query_blk, key_blk, value_blk, prefix, early_decay, decay_matrix)
        attention = attention.reshape(TOK_DEV, H * DH)
        gate_value = jax.nn.sigmoid(gate_blk.astype(jnp.float32))
        grad_float = cot_blk.astype(jnp.float32)
        grad_normed = grad_float * norm_gain * gate_value
        squares = lax.optimization_barrier(jnp.sum(attention * attention, axis=1))
        crossed = lax.optimization_barrier(jnp.sum(grad_normed * attention, axis=1))
        inverse = lax.rsqrt(squares / HD + norm_eps)[:, None]
        normed = attention * inverse
        grad_gate = (grad_float * normed * norm_gain * gate_value * (1.0 - gate_value)).astype(jnp.bfloat16)
        gain_term = lax.optimization_barrier(jnp.sum(grad_float * normed * gate_value, axis=0))
        grad_attention = (inverse * (grad_normed - normed * inverse * crossed[:, None] / HD)).astype(jnp.bfloat16)
        grad_heads = grad_attention.reshape(TOK_DEV, H, DH)
        ahead_sum = jnp.einsum('thd,the->hde', early_decay[:, :, None] * query_blk.astype(jnp.float32), grad_heads.astype(jnp.float32), precision=lax.Precision.HIGHEST)
        return (grad_gate, gain_term, grad_heads, ahead_sum)
    grad_gate, gain_terms, grad_blocks, ahead_sums = lax.map(norm_block, (query_blocks, key_blocks, value_blocks, gate_blocks, cot_blocks, prefixes))
    grad_gain = lax.optimization_barrier(jnp.sum(gain_terms, axis=0))
    _, suffixes = lax.scan(step_state, jnp.zeros((H, DH, DH), jnp.float32), ahead_sums, reverse=True)

    def grad_block(items):
        query_blk, key_blk, value_blk, grad_heads, prefix, suffix = items
        _, attn_weights = forward_block(query_blk, key_blk, value_blk, prefix, early_decay, decay_matrix)
        grad_f = grad_heads.astype(jnp.float32)
        grad_scores = (jnp.einsum('the,she->hts', grad_f, value_blk.astype(jnp.float32)) * decay_matrix).astype(jnp.bfloat16)
        score_f = grad_scores.astype(jnp.float32)
        grad_q = jnp.einsum('hts,shd->thd', score_f, key_blk.astype(jnp.float32))
        grad_q = grad_q + early_decay[:, :, None] * jnp.einsum('the,hde->thd', grad_f, prefix, precision=lax.Precision.HIGHEST) / DH
        grad_k = jnp.einsum('hts,thd->shd', score_f, query_blk.astype(jnp.float32))
        grad_k = grad_k + late_decay[:, :, None] * jnp.einsum('she,hde->shd', value_blk.astype(jnp.float32), suffix, precision=lax.Precision.HIGHEST) / DH
        grad_v = jnp.einsum('hts,the->she', attn_weights.astype(jnp.float32), grad_f)
        grad_v = grad_v + late_decay[:, :, None] * jnp.einsum('shd,hde->she', key_blk.astype(jnp.float32), suffix, precision=lax.Precision.HIGHEST) / DH
        return (grad_q.astype(jnp.bfloat16), grad_k.astype(jnp.bfloat16), grad_v.astype(jnp.bfloat16))
    grad_q, grad_k, grad_v = lax.map(grad_block, (query_blocks, key_blocks, value_blocks, grad_blocks, prefixes, suffixes))
    shape_out = (TOKENS, H * DH)
    return (grad_q.reshape(shape_out), grad_k.reshape(shape_out), grad_v.reshape(shape_out), grad_gate.reshape(shape_out), grad_gain)
```

```python
import jax
import jax.numpy as jnp
from jax import lax
from jax.sharding import PartitionSpec as P

DH = 128
HD = 8192


rate_unit = 2.0 ** (-20)
norm_eps = 1e-06


def swap(array, axis):
    return lax.all_to_all(array, axis, 0, 0)


def scan_table(span_rate, members, backward):
    block = jnp.arange(members, dtype=jnp.float32)
    gap = block[:, None] - block[None, :]
    gap = (-gap if backward else gap) - 1.0
    return jnp.where(gap >= 0.0, jnp.exp(-span_rate * jnp.maximum(gap, 0.0)), 0.0)


def body(queries, key_rows, value_rows, gate_in, grad_out, decay_ints, norm_gain):
    row_count, feature_count = queries.shape
    head_count = feature_count // DH
    members = lax.axis_size("ctx")
    rows = head_count * DH // members
    decay_rate = decay_ints.astype(jnp.float32) * rate_unit
    owned_head = lax.axis_index("ctx") * rows // DH
    span_rate = lax.dynamic_index_in_dim(decay_rate, owned_head, keepdims=False) * row_count
    positions = jnp.arange(row_count, dtype=jnp.float32)
    early_decay = jnp.exp(-decay_rate[None, :] * (positions[:, None] + 1.0))
    late_decay = jnp.exp(-decay_rate[None, :] * (row_count - 1.0 - positions[:, None]))
    distance = positions[:, None] - positions[None, :]
    decay_matrix = (
        jnp.where(
            distance[None] >= 0.0,
            jnp.exp(-decay_rate[:, None, None] * jnp.maximum(distance, 0.0)[None]),
            0.0,
        )
        / DH
    )
    q_heads = queries.reshape(row_count, head_count, DH)
    k_heads = key_rows.reshape(row_count, head_count, DH)
    v_heads = value_rows.reshape(row_count, head_count, DH)
    highest = lax.Precision.HIGHEST
    summary = jnp.einsum(
        "shd,she->hde",
        late_decay[:, :, None] * k_heads.astype(jnp.float32),
        v_heads.astype(jnp.float32),
        precision=highest,
    )
    there = swap(summary.reshape(members, rows, DH), "ctx")
    scanned = jnp.einsum(
        "cb,brl->crl", scan_table(span_rate, members, False), there, precision=highest
    )
    prefix = swap(scanned, "ctx").reshape(head_count, DH, DH)
    scores = jnp.einsum("thd,shd->hts", q_heads, k_heads, preferred_element_type=jnp.float32)
    attn_weights = (scores * decay_matrix).astype(jnp.bfloat16)
    attention = jnp.einsum(
        "hts,she->the", attn_weights, v_heads, preferred_element_type=jnp.float32
    )
    carried = jnp.einsum("thd,hde->the", q_heads.astype(jnp.float32), prefix, precision=highest)
    attention = (attention + early_decay[:, :, None] * carried / DH).reshape(
        row_count, feature_count
    )
    gate_value = jax.nn.sigmoid(gate_in.astype(jnp.float32))
    grad_float = grad_out.astype(jnp.float32)
    grad_normed = grad_float * norm_gain * gate_value
    stats = jnp.stack(
        [jnp.sum(attention * attention, axis=1), jnp.sum(grad_normed * attention, axis=1)]
    )
    head_members = lax.axis_size("head")
    stats = jnp.sum(swap(jnp.broadcast_to(stats, (head_members, 2, row_count)), "head"), axis=0)
    squares, crossed = stats[0], stats[1]
    inverse = lax.rsqrt(squares / HD + norm_eps)[:, None]
    normed = attention * inverse
    grad_gate = (grad_float * normed * norm_gain * gate_value * (1.0 - gate_value)).astype(
        jnp.bfloat16
    )
    gain_part = jnp.sum(grad_float * normed * gate_value, axis=0).reshape(1, head_count, DH)
    gain_rows = jnp.broadcast_to(gain_part, (members // head_count, head_count, DH))
    grad_attention = (inverse * (grad_normed - normed * inverse * crossed[:, None] / HD)).astype(
        jnp.bfloat16
    )
    grad_heads = grad_attention.reshape(row_count, head_count, DH)
    grad_wide = grad_heads.astype(jnp.float32)
    ahead_sum = jnp.einsum(
        "thd,the->hde",
        early_decay[:, :, None] * q_heads.astype(jnp.float32),
        grad_wide,
        precision=highest,
    )
    message = jnp.concatenate(
        [ahead_sum.reshape(members, rows, DH), gain_rows.reshape(members, 1, DH)], axis=1
    )
    there = swap(message[:, :, None, :], "ctx")[:, :, 0, :]
    scanned = jnp.einsum(
        "cb,brl->crl", scan_table(span_rate, members, True), there[:, :rows], precision=highest
    )
    gain_sum = jnp.broadcast_to(jnp.sum(there[:, rows:], axis=0)[None], (members, 1, DH))
    message = jnp.concatenate([scanned, gain_sum], axis=1)
    back = swap(message[:, :, None, :], "ctx")[:, :, 0, :]
    suffix = back[:, :rows].reshape(head_count, DH, DH)
    grad_gain = back[:head_count, rows].reshape(feature_count)
    grad_scores = (
        jnp.einsum("the,she->hts", grad_heads, v_heads, preferred_element_type=jnp.float32)
        * decay_matrix
    ).astype(jnp.bfloat16)
    grad_q = jnp.einsum("hts,shd->thd", grad_scores, k_heads, preferred_element_type=jnp.float32)
    grad_q = (
        grad_q
        + early_decay[:, :, None]
        * jnp.einsum("the,hde->thd", grad_wide, prefix, precision=highest)
        / DH
    )
    grad_k = jnp.einsum("hts,thd->shd", grad_scores, q_heads, preferred_element_type=jnp.float32)
    grad_k = (
        grad_k
        + late_decay[:, :, None]
        * jnp.einsum("she,hde->shd", v_heads.astype(jnp.float32), suffix, precision=highest)
        / DH
    )
    grad_v = jnp.einsum(
        "hts,the->she", attn_weights, grad_heads, preferred_element_type=jnp.float32
    )
    grad_v = (
        grad_v
        + late_decay[:, :, None]
        * jnp.einsum("shd,hde->she", k_heads.astype(jnp.float32), suffix, precision=highest)
        / DH
    )
    shape_out = (row_count, feature_count)
    return (
        grad_q.reshape(shape_out).astype(jnp.bfloat16),
        grad_k.reshape(shape_out).astype(jnp.bfloat16),
        grad_v.reshape(shape_out).astype(jnp.bfloat16),
        grad_gate,
        grad_gain,
    )


def solution(mesh):
    placed = (
        P("ctx", "head"),
        P("ctx", "head"),
        P("ctx", "head"),
        P("ctx", "head"),
        P("ctx", "head"),
        P("head"),
        P("head"),
    )
    return jax.shard_map(
        body,
        mesh=mesh,
        in_specs=placed,
        out_specs=(
            P("ctx", "head"),
            P("ctx", "head"),
            P("ctx", "head"),
            P("ctx", "head"),
            P("head"),
        ),
        check_vma=False,
    )
```

```python
import jax
import jax.numpy as jnp
from jax import lax
from jax.experimental import pallas as pl
from jax.experimental.pallas import tpu as pltpu
from jax.sharding import PartitionSpec as P

DH = 128
HD = 8192


rate_unit = 2.0 ** (-20)
norm_eps = 1e-06
wide = jnp.float32
half = jnp.bfloat16


def swap(array, axis):
    return lax.all_to_all(array, axis, 0, 0)


def halves(array, axis):
    high = array.astype(half)
    low = (array - high.astype(wide)).astype(half)
    return jnp.concatenate([high, low], axis=axis)


def twice(array, axis):
    return jnp.concatenate([array, array], axis=axis)


def dot(left, right):
    return jnp.dot(left, right, preferred_element_type=wide)


def dot_nt(left, right):
    return lax.dot_general(left, right, (((1,), (1,)), ((), ())), preferred_element_type=wide)


def dot_tn(left, right):
    return lax.dot_general(left, right, (((0,), (0,)), ((), ())), preferred_element_type=wide)


def rate_of(ints_ref, head):
    return ints_ref[head].astype(wide) * rate_unit


def decay_column(rate, rows, late):
    place = lax.broadcasted_iota(jnp.int32, (rows, DH), 0).astype(wide)
    return jnp.exp(-rate * ((rows - 1.0 - place) if late else (place + 1.0)))


def decay_square(rate, rows):
    later = lax.broadcasted_iota(jnp.int32, (rows, rows), 0)
    sooner = lax.broadcasted_iota(jnp.int32, (rows, rows), 1)
    gap = (later - sooner).astype(wide)
    return jnp.where(gap >= 0.0, jnp.exp(-rate * jnp.maximum(gap, 0.0)), 0.0) * (1.0 / DH)


def cols(head):
    return slice(head * DH, (head + 1) * DH)


def summary_kernel(ints_ref, k_ref, v_ref, out_ref):
    rows, features = k_ref.shape
    for head in range(features // DH):
        late = decay_column(rate_of(ints_ref, head), rows, True)
        values = late * v_ref[:, cols(head)].astype(wide)
        keys = twice(k_ref[:, cols(head)].T, 1)
        out_ref[cols(head), :] = dot(keys, halves(values, 0))


def owned_span(ints_ref, chunk, rows):
    owner = lax.axis_index("ctx") * chunk // DH
    return jnp.exp(jnp.full((1, DH), -rate_of(ints_ref, owner) * rows, wide))


def forward_kernel(members, rows, ints_ref, in_ref, out_ref):
    chunk = in_ref.shape[0] // members
    span = owned_span(ints_ref, chunk, rows)
    state = jnp.zeros((chunk, DH), wide)
    for block in range(members):
        out_ref[block * chunk : (block + 1) * chunk, :] = state
        state = span * state + in_ref[block * chunk : (block + 1) * chunk, :]


def backward_kernel(members, rows, ints_ref, in_ref, out_ref):
    step = in_ref.shape[0] // members
    chunk = step - 1
    span = owned_span(ints_ref, chunk, rows)
    state = jnp.zeros((chunk, DH), wide)
    gains = [jnp.zeros((1, DH), wide)] * 4
    for block in reversed(range(members)):
        out_ref[block * step : block * step + chunk, :] = state
        state = span * state + in_ref[block * step : block * step + chunk, :]
        gains[block % 4] = gains[block % 4] + in_ref[block * step + chunk : (block + 1) * step, :]
    gain = (gains[0] + gains[1]) + (gains[2] + gains[3])
    for block in range(members):
        out_ref[block * step + chunk : (block + 1) * step, :] = gain


def local_kernel(ints_ref, q_ref, k_ref, v_ref, gate_ref, grad_ref, local_ref, weights_ref, gated_ref, qt_ref):
    rows, features = q_ref.shape
    for head in range(features // DH):
        at = cols(head)
        scores = dot_nt(q_ref[:, at], k_ref[:, at])
        weights = (scores * decay_square(rate_of(ints_ref, head), rows)).astype(half)
        weights_ref[:, at] = weights
        local_ref[:, at] = dot(weights, v_ref[:, at])
        qt_ref[at, :] = q_ref[:, at].T
        gated_ref[:, at] = grad_ref[:, at].astype(wide) * jax.nn.sigmoid(gate_ref[:, at].astype(wide))


def attend_kernel(ints_ref, q_ref, prefix_ref, local_ref, gated_ref, gain_ref, attention_ref, stats_ref):
    rows, features = q_ref.shape
    squares = jnp.zeros((rows, DH), wide)
    crossed = jnp.zeros((rows, DH), wide)
    for head in range(features // DH):
        at = cols(head)
        early = decay_column(rate_of(ints_ref, head), rows, False) * (1.0 / DH)
        carried = dot(twice(q_ref[:, at], 1), halves(prefix_ref[at, :], 0))
        attention = local_ref[:, at] + early * carried
        attention_ref[:, at] = attention
        squares = squares + attention * attention
        crossed = crossed + gated_ref[:, at] * gain_ref[:, at] * attention
    squares = jnp.sum(squares.T, axis=0, keepdims=True)
    crossed = jnp.sum(crossed.T, axis=0, keepdims=True)
    line = lax.broadcasted_iota(jnp.int32, (8, DH), 0)
    pair = jnp.where(line == 0, squares, jnp.where(line == 1, crossed, 0.0))
    for member in range(stats_ref.shape[0]):
        stats_ref[member] = pair


def token_scales(stats_ref):
    total = stats_ref[0]
    for member in range(1, stats_ref.shape[0]):
        total = total + stats_ref[member]
    inverse = lax.rsqrt(total[0:1] * (1.0 / HD) + norm_eps)
    pull = inverse * inverse * inverse * total[1:2] * (1.0 / HD)
    line = lax.broadcasted_iota(jnp.int32, (8, DH), 0)
    columns = jnp.where(line == 0, inverse, jnp.where(line == 1, pull, 0.0)).T
    return columns[:, 0:1], columns[:, 1:2]


def ahead_kernel(members, ints_ref, stats_ref, attention_ref, gated_ref, gain_ref, qt_ref, grad_ref, out_ref):
    rows, features = attention_ref.shape
    heads = features // DH
    step = out_ref.shape[0] // members
    chunk = step - 1
    inverse, pull = token_scales(stats_ref)
    for head in range(heads):
        at = cols(head)
        early = decay_column(rate_of(ints_ref, head), rows, False)
        gated = gated_ref[:, at]
        attention = attention_ref[:, at]
        grad = (inverse * (gated * gain_ref[:, at]) - pull * attention).astype(half)
        grad_ref[:, at] = grad
        ahead = dot(twice(qt_ref[at, :], 1), halves(early * grad.astype(wide), 0))
        for piece in range(DH // chunk):
            block = head * (DH // chunk) + piece
            out_ref[block * step : block * step + chunk, :] = ahead[piece * chunk : (piece + 1) * chunk, :]
        gain_row = jnp.sum(gated * (attention * inverse), axis=0, keepdims=True)
        for block in range(head, members, heads):
            out_ref[block * step + chunk : (block + 1) * step, :] = gain_row


def early_grads_kernel(
    ints_ref, stats_ref, attention_ref, gated_ref, gain_ref, gate_ref, grad_ref, q_ref, k_ref, v_ref,
    weights_ref, prefix_ref, grad_q_ref, grad_gate_ref, local_k_ref, local_v_ref,
):
    rows, features = q_ref.shape
    inverse, _ = token_scales(stats_ref)
    for head in range(features // DH):
        at = cols(head)
        rate = rate_of(ints_ref, head)
        normed = attention_ref[:, at] * inverse
        rest = 1.0 - jax.nn.sigmoid(gate_ref[:, at].astype(wide))
        grad_gate_ref[:, at] = (gated_ref[:, at] * normed * gain_ref[:, at] * rest).astype(half)
        grad = grad_ref[:, at]
        grad_scores = (dot_nt(grad, v_ref[:, at]) * decay_square(rate, rows)).astype(half)
        early = decay_column(rate, rows, False) * (1.0 / DH)
        carried = dot_nt(twice(grad, 1), halves(prefix_ref[at, :], 1))
        grad_q_ref[:, at] = (dot(grad_scores, k_ref[:, at]) + early * carried).astype(half)
        local_k_ref[:, at] = dot_tn(grad_scores, q_ref[:, at])
        local_v_ref[:, at] = dot_tn(weights_ref[:, at], grad)


def final_kernel(members, ints_ref, back_ref, k_ref, v_ref, local_k_ref, local_v_ref, grad_k_ref, grad_v_ref, gain_ref):
    rows, features = k_ref.shape
    heads = features // DH
    step = back_ref.shape[0] // members
    chunk = step - 1
    pieces = DH // chunk
    for head in range(heads):
        at = cols(head)
        late = decay_column(rate_of(ints_ref, head), rows, True) * (1.0 / DH)
        suffix = jnp.concatenate(
            [
                back_ref[block * step : block * step + chunk, :]
                for block in range(head * pieces, (head + 1) * pieces)
            ],
            axis=0,
        )
        high = suffix.astype(half)
        low = (suffix - high.astype(wide)).astype(half)
        carried_k = dot_nt(twice(v_ref[:, at], 1), jnp.concatenate([high, low], axis=1))
        carried_v = dot(twice(k_ref[:, at], 1), jnp.concatenate([high, low], axis=0))
        grad_k_ref[:, at] = (local_k_ref[:, at] + late * carried_k).astype(half)
        grad_v_ref[:, at] = (local_v_ref[:, at] + late * carried_v).astype(half)
        gain_ref[:, at] = back_ref[head * step + chunk : (head + 1) * step, :]


def call(kernel, name, shapes, *operands, flops=0, bytes_moved=0):
    vmem = pl.BlockSpec(memory_space=pltpu.VMEM)
    in_specs = [pl.BlockSpec(memory_space=pltpu.SMEM)] + [vmem] * (len(operands) - 1)
    many = isinstance(shapes, (list, tuple))
    out_shape = [jax.ShapeDtypeStruct(*shape) for shape in shapes]
    results = pl.pallas_call(
        kernel,
        out_shape=out_shape,
        in_specs=in_specs,
        out_specs=[vmem] * len(out_shape),
        compiler_params=pltpu.CompilerParams(vmem_limit_bytes=24 * 1024 * 1024),
        cost_estimate=pl.CostEstimate(flops=flops, bytes_accessed=bytes_moved, transcendentals=0),
        name=name,
    )(*operands)
    return results if len(out_shape) > 1 else results[0]


def body(queries, key_rows, value_rows, gate_in, grad_out, decay_ints, norm_gain):
    rows, features = queries.shape
    heads = features // DH
    members = lax.axis_size("ctx")
    head_members = lax.axis_size("head")
    chunk = features // members
    step = chunk + 1
    gain = norm_gain.reshape(1, features)
    square = rows * features
    flat = ((features, DH), wide)
    long = ((members * step, DH), wide)

    def across(array, width):
        shape = (members, width, DH) if width % 8 == 0 else (members, width, 1, DH)
        return swap(array.reshape(shape), "ctx").reshape(members * width, DH)

    summary = call(summary_kernel, "summary", [flat], decay_ints, key_rows, value_rows)
    there = across(summary, chunk)
    local, weights, gated, queries_t = call(
        local_kernel,
        "local_attention",
        [((rows, features), wide), ((rows, features), half), ((rows, features), wide), ((features, rows), half)],
        decay_ints, queries, key_rows, value_rows, gate_in, grad_out,
        flops=8 * square * DH, bytes_moved=20 * square,
    )

    def forward(*refs):
        forward_kernel(members, rows, *refs)

    prefix = across(call(forward, "forward_scan", [flat], decay_ints, there), chunk)
    attention, stats = call(
        attend_kernel,
        "attend",
        [((rows, features), wide), ((head_members, 8, rows), wide)],
        decay_ints, queries, prefix, local, gated, gain,
    )
    stats = swap(stats, "head")

    def ahead(*refs):
        ahead_kernel(members, *refs)

    grad, message = call(
        ahead,
        "ahead",
        [((rows, features), half), long],
        decay_ints, stats, attention, gated, gain, queries_t,
    )
    there = across(message, step)
    grad_q, grad_gate, local_k, local_v = call(
        early_grads_kernel,
        "early_grads",
        [((rows, features), half), ((rows, features), half), ((rows, features), wide), ((rows, features), wide)],
        decay_ints, stats, attention, gated, gain, gate_in, grad, queries, key_rows, value_rows,
        weights, prefix,
        flops=20 * square * DH, bytes_moved=24 * square,
    )

    def backward(*refs):
        backward_kernel(members, rows, *refs)

    back = across(call(backward, "backward_scan", [long], decay_ints, there), step)

    def final(*refs):
        final_kernel(members, *refs)

    grad_k, grad_v, grad_gain = call(
        final,
        "final",
        [((rows, features), half), ((rows, features), half), ((1, features), wide)],
        decay_ints, back, key_rows, value_rows, local_k, local_v,
    )
    return grad_q, grad_k, grad_v, grad_gate, grad_gain.reshape(features)


def solution(mesh):
    placed = (
        P("ctx", "head"),
        P("ctx", "head"),
        P("ctx", "head"),
        P("ctx", "head"),
        P("ctx", "head"),
        P("head"),
        P("head"),
    )
    return jax.shard_map(
        body,
        mesh=mesh,
        in_specs=placed,
        out_specs=(
            P("ctx", "head"),
            P("ctx", "head"),
            P("ctx", "head"),
            P("ctx", "head"),
            P("head"),
        ),
        check_vma=False,
    )
```

```python
import functools

import jax
import jax.numpy as jnp
from jax import lax
from jax.experimental import pallas as pl
from jax.experimental.pallas import tpu as pltpu
from jax.sharding import PartitionSpec as P

DH = 128
HD = 8192


rate_unit = 2.0 ** (-20)
norm_eps = 1e-06
wide = jnp.float32
half = jnp.bfloat16


def swap(array, axis):
    return lax.all_to_all(array, axis, 0, 0)


def halves(array, axis):
    high = array.astype(half)
    low = (array - high.astype(wide)).astype(half)
    return jnp.concatenate([high, low], axis=axis)


def twice(array, axis):
    return jnp.concatenate([array, array], axis=axis)


def dot(left, right):
    return jnp.dot(left, right, preferred_element_type=wide)


def dot_nt(left, right):
    return lax.dot_general(left, right, (((1,), (1,)), ((), ())), preferred_element_type=wide)


def dot_tn(left, right):
    return lax.dot_general(left, right, (((0,), (0,)), ((), ())), preferred_element_type=wide)


def rate_of(ints_ref, head):
    return ints_ref[head].astype(wide) * rate_unit


def decay_column(rate, rows, late):
    place = lax.broadcasted_iota(jnp.int32, (rows, DH), 0).astype(wide)
    return jnp.exp(-rate * ((rows - 1.0 - place) if late else (place + 1.0)))


def decay_square(rate, rows):
    later = lax.broadcasted_iota(jnp.int32, (rows, rows), 0)
    sooner = lax.broadcasted_iota(jnp.int32, (rows, rows), 1)
    gap = (later - sooner).astype(wide)
    return jnp.where(gap >= 0.0, jnp.exp(-rate * jnp.maximum(gap, 0.0)), 0.0) * (1.0 / DH)


def cols(head):
    return slice(head * DH, (head + 1) * DH)


def summary_kernel(members, ints_ref, k_ref, v_ref, out_ref, spans_ref, ints, keys, values, arrived):
    rows, features = k_ref.shape
    heads = features // DH
    copies = [
        pltpu.make_async_copy(source, target, arrived.at[number])
        for number, (source, target) in enumerate(((ints_ref, ints), (k_ref, keys), (v_ref, values)))
    ]
    for copy in copies:
        copy.start()
    for copy in copies:
        copy.wait()
    for head in range(heads):
        late = decay_column(rate_of(ints, head), rows, True)
        weighted = late * values[:, cols(head)].astype(wide)
        out_ref[cols(head), :] = dot(twice(keys[:, cols(head)].T, 1), halves(weighted, 0))
    owned = lax.axis_index("ctx") * (features // members) // DH
    power = lax.broadcasted_iota(jnp.int32, (8, DH), 0).astype(wide) + 1.0
    spans_ref[0:8, :] = jnp.exp(-(rate_of(ints, owned) * rows) * power)
    for head in range(heads):
        spans_ref[8 + head : 9 + head, :] = jnp.full((1, DH), rate_of(ints, head), wide)


def scan_blocks(order, span, leap, take, put, zero):
    chains = [order[at : at + 8] for at in range(0, len(order), 8)]
    totals = []
    for chain in chains:
        state = take(chain[0])
        for block in chain[1:]:
            state = span * state + take(block)
        totals.append(state)
    starts = [zero]
    for total in totals[:-1]:
        starts.append(leap * starts[-1] + total)
    for chain, state in zip(chains, starts):
        for block in chain:
            put(block, state)
            state = span * state + take(block)


def forward_kernel(members, spans_ref, in_ref, out_ref):
    chunk = in_ref.shape[0] // members

    def take(block):
        return in_ref[block * chunk : (block + 1) * chunk, :]

    def put(block, state):
        out_ref[block * chunk : (block + 1) * chunk, :] = state

    order = list(range(members))
    scan_blocks(order, spans_ref[0:1, :], spans_ref[7:8, :], take, put, jnp.zeros((chunk, DH), wide))


def backward_kernel(members, spans_ref, in_ref, out_ref):
    step = in_ref.shape[0] // members
    chunk = step - 1

    def take(block):
        return in_ref[block * step : block * step + chunk, :]

    def put(block, state):
        out_ref[block * step : block * step + chunk, :] = state

    order = list(reversed(range(members)))
    scan_blocks(order, spans_ref[0:1, :], spans_ref[7:8, :], take, put, jnp.zeros((chunk, DH), wide))
    gains = [in_ref[block * step + chunk : (block + 1) * step, :] for block in range(members)]
    while len(gains) > 1:
        gains = [gains[at] + gains[at + 1] for at in range(0, len(gains), 2)]
    for block in range(members):
        out_ref[block * step + chunk : (block + 1) * step, :] = gains[0]


def local_kernel(
    spans_ref, q_ref, k_ref, v_ref, gate_ref, grad_ref, gain_ref,
    local_ref, weights_ref, gated_ref, scaled_ref, qt_ref, early_ref, late_ref,
):
    rows, features = q_ref.shape
    for head in range(features // DH):
        at = cols(head)
        rate = spans_ref[8 + head : 9 + head, :]
        scores = dot_nt(q_ref[:, at], k_ref[:, at])
        weights = (scores * decay_square(rate, rows)).astype(half)
        weights_ref[:, at] = weights
        local_ref[:, at] = dot(weights, v_ref[:, at])
        qt_ref[at, :] = q_ref[:, at].T
        gated = grad_ref[:, at].astype(wide) * jax.nn.sigmoid(gate_ref[:, at].astype(wide))
        gated_ref[:, at] = gated
        scaled_ref[:, at] = gated * gain_ref[:, at]
        early_ref[:, at] = decay_column(rate, rows, False)
        late_ref[:, at] = decay_column(rate, rows, True) * (1.0 / DH)


def attend_kernel(q_ref, prefix_ref, local_ref, scaled_ref, early_ref, attention_ref, stats_ref):
    rows, features = q_ref.shape
    squares = jnp.zeros((rows, DH), wide)
    crossed = jnp.zeros((rows, DH), wide)
    for head in range(features // DH):
        at = cols(head)
        carried = dot(twice(q_ref[:, at], 1), halves(prefix_ref[at, :], 0)) * (1.0 / DH)
        attention = local_ref[:, at] + early_ref[:, at] * carried
        attention_ref[:, at] = attention
        squares = squares + attention * attention
        crossed = crossed + scaled_ref[:, at] * attention
    squares = jnp.sum(squares.T, axis=0, keepdims=True)
    crossed = jnp.sum(crossed.T, axis=0, keepdims=True)
    line = lax.broadcasted_iota(jnp.int32, (8, DH), 0)
    pair = jnp.where(line == 0, squares, jnp.where(line == 1, crossed, 0.0))
    for member in range(stats_ref.shape[0]):
        stats_ref[member] = pair


def token_scales(stats_ref):
    total = stats_ref[0]
    for member in range(1, stats_ref.shape[0]):
        total = total + stats_ref[member]
    inverse = lax.rsqrt(total[0:1] * (1.0 / HD) + norm_eps)
    pull = inverse * inverse * inverse * total[1:2] * (1.0 / HD)
    line = lax.broadcasted_iota(jnp.int32, (8, DH), 0)
    columns = jnp.where(line == 0, inverse, jnp.where(line == 1, pull, 0.0)).T
    return columns[:, 0:1], columns[:, 1:2]


def ahead_kernel(
    members, stats_ref, attention_ref, gated_ref, scaled_ref, qt_ref, early_ref, grad_ref, out_ref
):
    rows, features = attention_ref.shape
    heads = features // DH
    step = out_ref.shape[0] // members
    chunk = step - 1
    inverse, pull = token_scales(stats_ref)
    for head in range(heads):
        at = cols(head)
        attention = attention_ref[:, at]
        grad = (inverse * scaled_ref[:, at] - pull * attention).astype(half)
        grad_ref[:, at] = grad
        ahead = dot(twice(qt_ref[at, :], 1), halves(early_ref[:, at] * grad.astype(wide), 0))
        for piece in range(DH // chunk):
            start = (head * (DH // chunk) + piece) * step
            out_ref[start : start + chunk, :] = ahead[piece * chunk : (piece + 1) * chunk, :]
        gain_row = jnp.sum(gated_ref[:, at] * (attention * inverse), axis=0, keepdims=True)
        for block in range(head, members, heads):
            out_ref[block * step + chunk : (block + 1) * step, :] = gain_row


def early_grads_kernel(
    spans_ref, stats_ref, attention_ref, scaled_ref, gate_ref, grad_ref, q_ref, k_ref, v_ref,
    weights_ref, prefix_ref, early_ref, grad_q_ref, grad_gate_ref, local_k_ref, local_v_ref,
):
    rows, features = q_ref.shape
    inverse, _ = token_scales(stats_ref)
    for head in range(features // DH):
        at = cols(head)
        normed = attention_ref[:, at] * inverse
        rest = 1.0 - jax.nn.sigmoid(gate_ref[:, at].astype(wide))
        grad_gate_ref[:, at] = (scaled_ref[:, at] * normed * rest).astype(half)
        grad = grad_ref[:, at]
        square = decay_square(spans_ref[8 + head : 9 + head, :], rows)
        grad_scores = (dot_nt(grad, v_ref[:, at]) * square).astype(half)
        carried = dot_nt(twice(grad, 1), halves(prefix_ref[at, :], 1)) * (1.0 / DH)
        grad_q = dot(grad_scores, k_ref[:, at]) + early_ref[:, at] * carried
        grad_q_ref[:, at] = grad_q.astype(half)
        local_k_ref[:, at] = dot_tn(grad_scores, q_ref[:, at])
        local_v_ref[:, at] = dot_tn(weights_ref[:, at], grad)


def final_kernel(
    members, back_ref, k_ref, v_ref, local_k_ref, local_v_ref, late_ref, grad_k_ref, grad_v_ref, gain_ref,
    keys, values, gain, left,
):
    rows, features = k_ref.shape
    heads = features // DH
    copies = []

    def send(source, target):
        copy = pltpu.make_async_copy(source, target, left.at[len(copies)])
        copy.start()
        copies.append(copy)

    step = back_ref.shape[0] // members
    chunk = step - 1
    pieces = DH // chunk
    for head in range(heads):
        gain[:, cols(head)] = back_ref[head * step + chunk : (head + 1) * step, :]
    send(gain, gain_ref)
    for head in range(heads):
        at = cols(head)
        late = late_ref[:, at]
        starts = [block * step for block in range(head * pieces, (head + 1) * pieces)]
        suffix = jnp.concatenate([back_ref[start : start + chunk, :] for start in starts], axis=0)
        high = suffix.astype(half)
        low = (suffix - high.astype(wide)).astype(half)
        carried_k = dot_nt(twice(v_ref[:, at], 1), jnp.concatenate([high, low], axis=1))
        carried_v = dot(twice(k_ref[:, at], 1), jnp.concatenate([high, low], axis=0))
        keys[:, at] = (local_k_ref[:, at] + late * carried_k).astype(half)
        send(keys.at[:, at], grad_k_ref.at[:, at])
        values[:, at] = (local_v_ref[:, at] + late * carried_v).astype(half)
        send(values.at[:, at], grad_v_ref.at[:, at])
    for copy in copies:
        copy.wait()


def call(kernel, name, shapes, *operands, place=pltpu.VMEM, out_place=pltpu.VMEM, scratch=(), flops=0, bytes_moved=0):
    out_shape = [jax.ShapeDtypeStruct(*shape) for shape in shapes]
    results = pl.pallas_call(
        kernel,
        out_shape=out_shape,
        in_specs=[pl.BlockSpec(memory_space=place)] * len(operands),
        out_specs=[pl.BlockSpec(memory_space=out_place)] * len(out_shape),
        scratch_shapes=list(scratch),
        compiler_params=pltpu.CompilerParams(vmem_limit_bytes=24 * 1024 * 1024),
        cost_estimate=pl.CostEstimate(flops=flops, bytes_accessed=bytes_moved, transcendentals=0),
        name=name,
    )(*operands)
    return results if len(out_shape) > 1 else results[0]


def body(queries, key_rows, value_rows, gate_in, grad_out, decay_ints, norm_gain):
    rows, features = queries.shape
    members = lax.axis_size("ctx")
    head_members = lax.axis_size("head")
    chunk = features // members
    step = chunk + 1
    area = rows * features
    flat = ((features, DH), wide)
    long = ((members * step, DH), wide)
    block_wide = ((rows, features), wide)
    block_half = ((rows, features), half)

    def across(array, width):
        shape = (members, width, DH) if width % 8 == 0 else (members, width, 1, DH)
        return swap(array.reshape(shape), "ctx").reshape(members * width, DH)

    def sized(kernel):
        return functools.partial(kernel, members)

    summary, spans = call(
        sized(summary_kernel),
        "summary",
        [flat, ((16, DH), wide)],
        *[pltpu.with_memory_space_constraint(a, pltpu.HBM) for a in (decay_ints, key_rows, value_rows)],
        place=pltpu.HBM,
        scratch=[
            pltpu.SMEM(decay_ints.shape, jnp.int32),
            pltpu.VMEM((rows, features), half),
            pltpu.VMEM((rows, features), half),
            pltpu.SemaphoreType.DMA((3,)),
        ],
    )
    there = across(summary, chunk)
    local, weights, gated, scaled, queries_t, early, late = call(
        local_kernel,
        "local_attention",
        [block_wide, block_half, block_wide, block_wide, ((features, rows), half), block_wide, block_wide],
        spans, queries, key_rows, value_rows, gate_in, grad_out, norm_gain.reshape(1, features),
        flops=8 * area * DH, bytes_moved=28 * area,
    )
    prefix = across(call(sized(forward_kernel), "forward_scan", [flat], spans, there), chunk)
    attention, stats = call(
        attend_kernel,
        "attend",
        [block_wide, ((head_members, 8, rows), wide)],
        queries, prefix, local, scaled, early,
    )
    stats = swap(stats, "head")
    grad, message = call(
        sized(ahead_kernel),
        "ahead",
        [block_half, long],
        stats, attention, gated, scaled, queries_t, early,
    )
    there = across(message, step)
    grad_q, grad_gate, local_k, local_v = call(
        early_grads_kernel,
        "early_grads",
        [block_half, block_half, block_wide, block_wide],
        spans, stats, attention, scaled, gate_in, grad, queries, key_rows, value_rows,
        weights, prefix, early,
        flops=20 * area * DH, bytes_moved=28 * area,
    )
    back = across(call(sized(backward_kernel), "backward_scan", [long], spans, there), step)
    grad_k, grad_v, grad_gain = call(
        sized(final_kernel),
        "final",
        [block_half, block_half, ((1, features), wide)],
        back, key_rows, value_rows, local_k, local_v, late,
        out_place=pltpu.HBM,
        scratch=[
            pltpu.VMEM((rows, features), half),
            pltpu.VMEM((rows, features), half),
            pltpu.VMEM((1, features), wide),
            pltpu.SemaphoreType.DMA((2 * features // DH + 1,)),
        ],
    )
    return grad_q, grad_k, grad_v, grad_gate, grad_gain.reshape(features)


def solution(mesh):
    placed = (
        P("ctx", "head"),
        P("ctx", "head"),
        P("ctx", "head"),
        P("ctx", "head"),
        P("ctx", "head"),
        P("head"),
        P("head"),
    )
    return jax.shard_map(
        body,
        mesh=mesh,
        in_specs=placed,
        out_specs=(
            P("ctx", "head"),
            P("ctx", "head"),
            P("ctx", "head"),
            P("ctx", "head"),
            P("head"),
        ),
        check_vma=False,
    )
```

```python
import functools

import jax
import jax.numpy as jnp
from jax import lax
from jax.experimental import pallas as pl
from jax.experimental.pallas import tpu as pltpu
from jax.sharding import PartitionSpec as P

DH = 128
HD = 8192


rate_unit = 2.0 ** (-20)
norm_eps = 1e-06
SIDE = 8
wide = jnp.float32
half = jnp.bfloat16


def swap(array, axis, groups=None):
    return lax.all_to_all(array, axis, 0, 0, axis_index_groups=groups)


def halves(array, axis):
    high = array.astype(half)
    low = (array - high.astype(wide)).astype(half)
    return jnp.concatenate([high, low], axis=axis)


def twice(array, axis):
    return jnp.concatenate([array, array], axis=axis)


def dot(left, right):
    return jnp.dot(left, right, preferred_element_type=wide)


def dot_nt(left, right):
    return lax.dot_general(left, right, (((1,), (1,)), ((), ())), preferred_element_type=wide)


def dot_tn(left, right):
    return lax.dot_general(left, right, (((0,), (0,)), ((), ())), preferred_element_type=wide)


def rate_of(ints_ref, head):
    return ints_ref[head].astype(wide) * rate_unit


def decay_column(rate, rows, late):
    place = lax.broadcasted_iota(jnp.int32, (rows, DH), 0).astype(wide)
    return jnp.exp(-rate * ((rows - 1.0 - place) if late else (place + 1.0)))


def decay_square(rate, rows):
    later = lax.broadcasted_iota(jnp.int32, (rows, rows), 0)
    sooner = lax.broadcasted_iota(jnp.int32, (rows, rows), 1)
    gap = (later - sooner).astype(wide)
    return jnp.where(gap >= 0.0, jnp.exp(-rate * jnp.maximum(gap, 0.0)), 0.0) * (1.0 / DH)


def cols(head):
    return slice(head * DH, (head + 1) * DH)


def summary_kernel(members, ints_ref, k_ref, v_ref, out_ref, spans_ref, ints, keys, values, arrived):
    rows, features = k_ref.shape
    heads = features // DH
    copies = [
        pltpu.make_async_copy(source, target, arrived.at[number])
        for number, (source, target) in enumerate(((ints_ref, ints), (k_ref, keys), (v_ref, values)))
    ]
    for copy in copies:
        copy.start()
    for copy in copies:
        copy.wait()
    for head in range(heads):
        late = decay_column(rate_of(ints, head), rows, True)
        weighted = late * values[:, cols(head)].astype(wide)
        out_ref[cols(head), :] = dot(twice(keys[:, cols(head)].T, 1), halves(weighted, 0))
    place = lax.axis_index("ctx")
    line = lax.broadcasted_iota(jnp.int32, (8, DH), 0)
    owned = place * (features // members) // DH
    spans_ref[0:8, :] = jnp.exp(-(rate_of(ints, owned) * rows) * (line.astype(wide) + 1.0))
    for head in range(heads):
        spans_ref[8 + head : 9 + head, :] = jnp.full((1, DH), rate_of(ints, head), wide)
    side = SIDE
    across, down = place % side, place // side
    owned = across * (features // side) // DH
    span_rate = rate_of(ints, owned) * rows
    spans_ref[16:24, :] = jnp.exp(jnp.full((8, DH), -span_rate, wide))
    for at, gap in ((24, line - down - 1), (32, down - line - 1)):
        power = jnp.maximum(gap, 0).astype(wide) * side
        spans_ref[at : at + 8, :] = jnp.where(gap >= 0, jnp.exp(-span_rate * power), 0.0)


def add_up(terms):
    while len(terms) > 1:
        pairs = [terms[at] + terms[at + 1] for at in range(0, len(terms) - 1, 2)]
        terms = pairs + terms[2 * len(pairs) :]
    return terms[0]


def line_order(backward):
    return list(reversed(range(SIDE))) if backward else list(range(SIDE))


def line_total_kernel(backward, width, spans_ref, in_ref, out_ref):
    step = in_ref.shape[0] // SIDE
    span = spans_ref[16:17, :]
    state = None
    for block in line_order(backward):
        term = in_ref[block * step : block * step + width, :]
        state = term if state is None else span * state + term
    for block in range(SIDE):
        out_ref[block * step : block * step + width, :] = state
    if step > width:
        gain = add_up([in_ref[block * step + width : (block + 1) * step, :] for block in range(SIDE)])
        for block in range(SIDE):
            out_ref[block * step + width : (block + 1) * step, :] = gain


def line_scan_kernel(backward, width, spans_ref, totals_ref, in_ref, out_ref):
    step = in_ref.shape[0] // SIDE
    span = spans_ref[16:17, :]
    first = 24 if backward else 32
    state = add_up(
        [
            spans_ref[first + block : first + block + 1, :] * totals_ref[block * step : block * step + width, :]
            for block in range(SIDE)
        ]
    )
    for block in line_order(backward):
        out_ref[block * step : block * step + width, :] = state
        state = span * state + in_ref[block * step : block * step + width, :]
    if step > width:
        gain = add_up([totals_ref[block * step + width : (block + 1) * step, :] for block in range(SIDE)])
        for block in range(SIDE):
            out_ref[block * step + width : (block + 1) * step, :] = gain


def scan_blocks(order, span, leap, take, put, zero):
    chains = [order[at : at + 8] for at in range(0, len(order), 8)]
    totals = []
    for chain in chains:
        state = take(chain[0])
        for block in chain[1:]:
            state = span * state + take(block)
        totals.append(state)
    starts = [zero]
    for total in totals[:-1]:
        starts.append(leap * starts[-1] + total)
    for chain, state in zip(chains, starts):
        for block in chain:
            put(block, state)
            state = span * state + take(block)


def forward_kernel(members, spans_ref, in_ref, out_ref):
    chunk = in_ref.shape[0] // members

    def take(block):
        return in_ref[block * chunk : (block + 1) * chunk, :]

    def put(block, state):
        out_ref[block * chunk : (block + 1) * chunk, :] = state

    order = list(range(members))
    scan_blocks(order, spans_ref[0:1, :], spans_ref[7:8, :], take, put, jnp.zeros((chunk, DH), wide))


def local_kernel(
    spans_ref, q_ref, k_ref, v_ref, gate_ref, grad_ref, gain_ref,
    local_ref, weights_ref, gated_ref, scaled_ref, qt_ref, early_ref, late_ref,
):
    rows, features = q_ref.shape
    for head in range(features // DH):
        at = cols(head)
        rate = spans_ref[8 + head : 9 + head, :]
        scores = dot_nt(q_ref[:, at], k_ref[:, at])
        weights = (scores * decay_square(rate, rows)).astype(half)
        weights_ref[:, at] = weights
        local_ref[:, at] = dot(weights, v_ref[:, at])
        qt_ref[at, :] = q_ref[:, at].T
        gated = grad_ref[:, at].astype(wide) * jax.nn.sigmoid(gate_ref[:, at].astype(wide))
        gated_ref[:, at] = gated
        scaled_ref[:, at] = gated * gain_ref[:, at]
        early_ref[:, at] = decay_column(rate, rows, False)
        late_ref[:, at] = decay_column(rate, rows, True) * (1.0 / DH)


def attend_kernel(q_ref, prefix_ref, local_ref, scaled_ref, early_ref, attention_ref, stats_ref):
    rows, features = q_ref.shape
    squares = jnp.zeros((rows, DH), wide)
    crossed = jnp.zeros((rows, DH), wide)
    for head in range(features // DH):
        at = cols(head)
        carried = dot(twice(q_ref[:, at], 1), halves(prefix_ref[at, :], 0)) * (1.0 / DH)
        attention = local_ref[:, at] + early_ref[:, at] * carried
        attention_ref[:, at] = attention
        squares = squares + attention * attention
        crossed = crossed + scaled_ref[:, at] * attention
    squares = jnp.sum(squares.T, axis=0, keepdims=True)
    crossed = jnp.sum(crossed.T, axis=0, keepdims=True)
    line = lax.broadcasted_iota(jnp.int32, (8, DH), 0)
    pair = jnp.where(line == 0, squares, jnp.where(line == 1, crossed, 0.0))
    for member in range(stats_ref.shape[0]):
        stats_ref[member] = pair


def token_scales(stats_ref):
    total = stats_ref[0]
    for member in range(1, stats_ref.shape[0]):
        total = total + stats_ref[member]
    inverse = lax.rsqrt(total[0:1] * (1.0 / HD) + norm_eps)
    pull = inverse * inverse * inverse * total[1:2] * (1.0 / HD)
    line = lax.broadcasted_iota(jnp.int32, (8, DH), 0)
    columns = jnp.where(line == 0, inverse, jnp.where(line == 1, pull, 0.0)).T
    return columns[:, 0:1], columns[:, 1:2]


def ahead_kernel(
    stats_ref, attention_ref, gated_ref, scaled_ref, qt_ref, early_ref, grad_ref, out_ref
):
    rows, features = attention_ref.shape
    heads = features // DH
    step = out_ref.shape[0] // SIDE
    width = features // SIDE
    pieces = DH // width
    inverse, pull = token_scales(stats_ref)
    for head in range(heads):
        at = cols(head)
        attention = attention_ref[:, at]
        grad = (inverse * scaled_ref[:, at] - pull * attention).astype(half)
        grad_ref[:, at] = grad
        ahead = dot(twice(qt_ref[at, :], 1), halves(early_ref[:, at] * grad.astype(wide), 0))
        for piece in range(pieces):
            start = (head * pieces + piece) * step
            out_ref[start : start + width, :] = ahead[piece * width : (piece + 1) * width, :]
        gain_row = jnp.sum(gated_ref[:, at] * (attention * inverse), axis=0, keepdims=True)
        for block in range(head, SIDE, heads):
            out_ref[block * step + width : (block + 1) * step, :] = jnp.broadcast_to(gain_row, (step - width, DH))


def early_grads_kernel(
    spans_ref, stats_ref, attention_ref, scaled_ref, gate_ref, grad_ref, q_ref, k_ref, v_ref,
    weights_ref, prefix_ref, early_ref, grad_q_ref, grad_gate_ref, local_k_ref, local_v_ref,
):
    rows, features = q_ref.shape
    inverse, _ = token_scales(stats_ref)
    for head in range(features // DH):
        at = cols(head)
        normed = attention_ref[:, at] * inverse
        rest = 1.0 - jax.nn.sigmoid(gate_ref[:, at].astype(wide))
        grad_gate_ref[:, at] = (scaled_ref[:, at] * normed * rest).astype(half)
        grad = grad_ref[:, at]
        square = decay_square(spans_ref[8 + head : 9 + head, :], rows)
        grad_scores = (dot_nt(grad, v_ref[:, at]) * square).astype(half)
        carried = dot_nt(twice(grad, 1), halves(prefix_ref[at, :], 1)) * (1.0 / DH)
        grad_q = dot(grad_scores, k_ref[:, at]) + early_ref[:, at] * carried
        grad_q_ref[:, at] = grad_q.astype(half)
        local_k_ref[:, at] = dot_tn(grad_scores, q_ref[:, at])
        local_v_ref[:, at] = dot_tn(weights_ref[:, at], grad)


def final_kernel(
    back_ref, k_ref, v_ref, local_k_ref, local_v_ref, late_ref, grad_k_ref, grad_v_ref, gain_ref,
    keys, values, gain, left,
):
    rows, features = k_ref.shape
    heads = features // DH
    copies = []

    def send(source, target):
        copy = pltpu.make_async_copy(source, target, left.at[len(copies)])
        copy.start()
        copies.append(copy)

    step = back_ref.shape[0] // SIDE
    width = features // SIDE
    pieces = DH // width
    for head in range(heads):
        gain[:, cols(head)] = back_ref[head * step + width : head * step + width + 1, :]
    send(gain, gain_ref)
    for head in range(heads):
        at = cols(head)
        late = late_ref[:, at]
        starts = [block * step for block in range(head * pieces, (head + 1) * pieces)]
        suffix = jnp.concatenate([back_ref[start : start + width, :] for start in starts], axis=0)
        high = suffix.astype(half)
        low = (suffix - high.astype(wide)).astype(half)
        carried_k = dot_nt(twice(v_ref[:, at], 1), jnp.concatenate([high, low], axis=1))
        carried_v = dot(twice(k_ref[:, at], 1), jnp.concatenate([high, low], axis=0))
        keys[:, at] = (local_k_ref[:, at] + late * carried_k).astype(half)
        send(keys.at[:, at], grad_k_ref.at[:, at])
        values[:, at] = (local_v_ref[:, at] + late * carried_v).astype(half)
        send(values.at[:, at], grad_v_ref.at[:, at])
    for copy in copies:
        copy.wait()


def call(kernel, name, shapes, *operands, place=pltpu.VMEM, out_place=pltpu.VMEM, scratch=(), flops=0, bytes_moved=0):
    out_shape = [jax.ShapeDtypeStruct(*shape) for shape in shapes]
    results = pl.pallas_call(
        kernel,
        out_shape=out_shape,
        in_specs=[pl.BlockSpec(memory_space=place)] * len(operands),
        out_specs=[pl.BlockSpec(memory_space=out_place)] * len(out_shape),
        scratch_shapes=list(scratch),
        compiler_params=pltpu.CompilerParams(vmem_limit_bytes=24 * 1024 * 1024),
        cost_estimate=pl.CostEstimate(flops=flops, bytes_accessed=bytes_moved, transcendentals=0),
        name=name,
    )(*operands)
    return results if len(out_shape) > 1 else results[0]


def body(queries, key_rows, value_rows, gate_in, grad_out, decay_ints, norm_gain):
    rows, features = queries.shape
    members = lax.axis_size("ctx")
    head_members = lax.axis_size("head")
    chunk = features // members
    width = features // SIDE
    step = width + 8
    lanes = [[down * SIDE + across for across in range(SIDE)] for down in range(SIDE)]
    columns = [[down * SIDE + across for down in range(SIDE)] for across in range(SIDE)]
    area = rows * features
    flat = ((features, DH), wide)
    long = ((SIDE * step, DH), wide)
    block_wide = ((rows, features), wide)
    block_half = ((rows, features), half)

    def everywhere(array):
        return swap(array.reshape(members, -1, DH), "ctx").reshape(-1, DH)

    def along(array, groups):
        return swap(array.reshape(SIDE, -1, DH), "ctx", groups).reshape(-1, DH)

    def sized(kernel):
        return functools.partial(kernel, members)

    summary, spans = call(
        sized(summary_kernel),
        "summary",
        [flat, ((40, DH), wide)],
        *[pltpu.with_memory_space_constraint(a, pltpu.HBM) for a in (decay_ints, key_rows, value_rows)],
        place=pltpu.HBM,
        scratch=[
            pltpu.SMEM(decay_ints.shape, jnp.int32),
            pltpu.VMEM((rows, features), half),
            pltpu.VMEM((rows, features), half),
            pltpu.SemaphoreType.DMA((3,)),
        ],
    )
    there = everywhere(summary)
    local, weights, gated, scaled, queries_t, early, late = call(
        local_kernel,
        "local_attention",
        [block_wide, block_half, block_wide, block_wide, ((features, rows), half), block_wide, block_wide],
        spans, queries, key_rows, value_rows, gate_in, grad_out, norm_gain.reshape(1, features),
        flops=8 * area * DH, bytes_moved=28 * area,
    )
    prefix = everywhere(call(sized(forward_kernel), "forward_scan", [flat], spans, there))
    attention, stats = call(
        attend_kernel,
        "attend",
        [block_wide, ((head_members, 8, rows), wide)],
        queries, prefix, local, scaled, early,
    )
    stats = swap(stats, "head")
    grad, message = call(
        ahead_kernel,
        "ahead",
        [block_half, long],
        stats, attention, gated, scaled, queries_t, early,
    )
    there = along(message, lanes)
    total = call(functools.partial(line_total_kernel, True, width), "line_total", [long], spans, there)
    totals = along(total, columns)
    grad_q, grad_gate, local_k, local_v = call(
        early_grads_kernel,
        "early_grads",
        [block_half, block_half, block_wide, block_wide],
        spans, stats, attention, scaled, gate_in, grad, queries, key_rows, value_rows,
        weights, prefix, early,
        flops=20 * area * DH, bytes_moved=28 * area,
    )
    scanned = call(functools.partial(line_scan_kernel, True, width), "line_scan", [long], spans, totals, there)
    back = along(scanned, lanes)
    grad_k, grad_v, grad_gain = call(
        final_kernel,
        "final",
        [block_half, block_half, ((1, features), wide)],
        back, key_rows, value_rows, local_k, local_v, late,
        out_place=pltpu.HBM,
        scratch=[
            pltpu.VMEM((rows, features), half),
            pltpu.VMEM((rows, features), half),
            pltpu.VMEM((1, features), wide),
            pltpu.SemaphoreType.DMA((2 * features // DH + 1,)),
        ],
    )
    return grad_q, grad_k, grad_v, grad_gate, grad_gain.reshape(features)


def solution(mesh):
    placed = (
        P("ctx", "head"),
        P("ctx", "head"),
        P("ctx", "head"),
        P("ctx", "head"),
        P("ctx", "head"),
        P("head"),
        P("head"),
    )
    return jax.shard_map(
        body,
        mesh=mesh,
        in_specs=placed,
        out_specs=(
            P("ctx", "head"),
            P("ctx", "head"),
            P("ctx", "head"),
            P("ctx", "head"),
            P("head"),
        ),
        check_vma=False,
    )
```

```python
import functools

import jax
import jax.numpy as jnp
from jax import lax
from jax.experimental import pallas as pl
from jax.experimental.pallas import tpu as pltpu
from jax.sharding import PartitionSpec as P

DH = 128
HD = 8192


rate_unit = 2.0 ** (-20)
norm_eps = 1e-06
wide = jnp.float32
half = jnp.bfloat16


def swap(array, axis):
    return lax.all_to_all(array, axis, 0, 0)


def halves(array, axis):
    high = array.astype(half)
    low = (array - high.astype(wide)).astype(half)
    return jnp.concatenate([high, low], axis=axis)


def twice(array, axis):
    return jnp.concatenate([array, array], axis=axis)


def dot(left, right):
    return jnp.dot(left, right, preferred_element_type=wide)


def dot_nt(left, right):
    return lax.dot_general(left, right, (((1,), (1,)), ((), ())), preferred_element_type=wide)


def dot_tn(left, right):
    return lax.dot_general(left, right, (((0,), (0,)), ((), ())), preferred_element_type=wide)


def rate_of(ints_ref, head):
    return ints_ref[head].astype(wide) * rate_unit


def decay_column(rate, rows, late):
    place = lax.broadcasted_iota(jnp.int32, (rows, DH), 0).astype(wide)
    return jnp.exp(-rate * ((rows - 1.0 - place) if late else (place + 1.0)))


def decay_square(rate, rows):
    later = lax.broadcasted_iota(jnp.int32, (rows, rows), 0)
    sooner = lax.broadcasted_iota(jnp.int32, (rows, rows), 1)
    gap = (later - sooner).astype(wide)
    return jnp.where(gap >= 0.0, jnp.exp(-rate * jnp.maximum(gap, 0.0)), 0.0) * (1.0 / DH)


def cols(head):
    return slice(head * DH, (head + 1) * DH)


def summary_kernel(members, ints_ref, k_ref, v_ref, out_ref, spans_ref, ints, keys, values, late, arrived):
    rows, features = k_ref.shape
    heads = features // DH
    copies = [
        pltpu.make_async_copy(source, target, arrived.at[number])
        for number, (source, target) in enumerate(((ints_ref, ints), (k_ref, keys), (v_ref, values)))
    ]
    for copy in copies:
        copy.start()
    copies[0].wait()
    owned = lax.axis_index("ctx") * (features // members) // DH
    power = lax.broadcasted_iota(jnp.int32, (8, DH), 0).astype(wide) + 1.0
    spans_ref[0:8, :] = jnp.exp(-(rate_of(ints, owned) * rows) * power)
    for head in range(heads):
        spans_ref[8 + head : 9 + head, :] = jnp.full((1, DH), rate_of(ints, head), wide)
        late[:, cols(head)] = decay_column(rate_of(ints, head), rows, True)
    copies[1].wait()
    copies[2].wait()
    for head in range(heads):
        weighted = late[:, cols(head)] * values[:, cols(head)].astype(wide)
        out_ref[cols(head), :] = dot(twice(keys[:, cols(head)].T, 1), halves(weighted, 0))


def scan_blocks(order, span, leap, take, put, zero):
    chains = [order[at : at + 8] for at in range(0, len(order), 8)]
    totals = [take(chain[0]) for chain in chains]
    for turn in range(1, 8):
        blocks = [take(chain[turn]) for chain in chains]
        totals = [span * total + block for total, block in zip(totals, blocks)]
    states = [zero]
    for total in totals[:-1]:
        states.append(leap * states[-1] + total)
    for turn in range(8):
        blocks = [take(chain[turn]) for chain in chains]
        for chain, state in zip(chains, states):
            put(chain[turn], state)
        states = [span * state + block for state, block in zip(states, blocks)]


def forward_kernel(members, spans_ref, in_ref, out_ref):
    chunk = in_ref.shape[0] // members

    def take(block):
        return in_ref[block * chunk : (block + 1) * chunk, :]

    def put(block, state):
        out_ref[block * chunk : (block + 1) * chunk, :] = state

    order = list(range(members))
    scan_blocks(order, spans_ref[0:1, :], spans_ref[7:8, :], take, put, jnp.zeros((chunk, DH), wide))


def backward_kernel(members, spans_ref, in_ref, out_ref):
    step = in_ref.shape[0] // members
    chunk = step - 1

    def take(block):
        return in_ref[block * step : block * step + chunk, :]

    def put(block, state):
        out_ref[block * step : block * step + chunk, :] = state

    order = list(reversed(range(members)))
    scan_blocks(order, spans_ref[0:1, :], spans_ref[7:8, :], take, put, jnp.zeros((chunk, DH), wide))
    gains = [in_ref[block * step + chunk : (block + 1) * step, :] for block in range(members)]
    while len(gains) > 1:
        gains = [gains[at] + gains[at + 1] for at in range(0, len(gains), 2)]
    for block in range(members):
        out_ref[block * step + chunk : (block + 1) * step, :] = gains[0]


def local_kernel(
    spans_ref, q_ref, k_ref, v_ref, gate_ref, grad_ref, gain_ref,
    local_ref, weights_ref, gated_ref, scaled_ref, qt_ref, early_ref, late_ref,
):
    rows, features = q_ref.shape
    for head in range(features // DH):
        at = cols(head)
        rate = spans_ref[8 + head : 9 + head, :]
        scores = dot_nt(q_ref[:, at], k_ref[:, at])
        weights = (scores * decay_square(rate, rows)).astype(half)
        weights_ref[:, at] = weights
        local_ref[:, at] = dot(weights, v_ref[:, at])
        qt_ref[at, :] = q_ref[:, at].T
        gated = grad_ref[:, at].astype(wide) * jax.nn.sigmoid(gate_ref[:, at].astype(wide))
        gated_ref[:, at] = gated
        scaled_ref[:, at] = gated * gain_ref[:, at]
        early_ref[:, at] = decay_column(rate, rows, False)
        late_ref[:, at] = decay_column(rate, rows, True) * (1.0 / DH)


def attend_kernel(q_ref, prefix_ref, local_ref, scaled_ref, early_ref, attention_ref, stats_ref):
    rows, features = q_ref.shape
    squares = jnp.zeros((rows, DH), wide)
    crossed = jnp.zeros((rows, DH), wide)
    for head in range(features // DH):
        at = cols(head)
        carried = dot(twice(q_ref[:, at], 1), halves(prefix_ref[at, :], 0)) * (1.0 / DH)
        attention = local_ref[:, at] + early_ref[:, at] * carried
        attention_ref[:, at] = attention
        squares = squares + attention * attention
        crossed = crossed + scaled_ref[:, at] * attention
    squares = jnp.sum(squares.T, axis=0, keepdims=True)
    crossed = jnp.sum(crossed.T, axis=0, keepdims=True)
    line = lax.broadcasted_iota(jnp.int32, (8, DH), 0)
    pair = jnp.where(line == 0, squares, jnp.where(line == 1, crossed, 0.0))
    for member in range(stats_ref.shape[0]):
        stats_ref[member] = pair


def token_scales(stats_ref):
    total = stats_ref[0]
    for member in range(1, stats_ref.shape[0]):
        total = total + stats_ref[member]
    inverse = lax.rsqrt(total[0:1] * (1.0 / HD) + norm_eps)
    pull = inverse * inverse * inverse * total[1:2] * (1.0 / HD)
    line = lax.broadcasted_iota(jnp.int32, (8, DH), 0)
    columns = jnp.where(line == 0, inverse, jnp.where(line == 1, pull, 0.0)).T
    return columns[:, 0:1], columns[:, 1:2]


def ahead_kernel(
    members, stats_ref, attention_ref, gated_ref, scaled_ref, qt_ref, early_ref, grad_ref, out_ref
):
    rows, features = attention_ref.shape
    heads = features // DH
    step = out_ref.shape[0] // members
    chunk = step - 1
    inverse, pull = token_scales(stats_ref)
    for head in range(heads):
        at = cols(head)
        attention = attention_ref[:, at]
        grad = (inverse * scaled_ref[:, at] - pull * attention).astype(half)
        grad_ref[:, at] = grad
        ahead = dot(twice(qt_ref[at, :], 1), halves(early_ref[:, at] * grad.astype(wide), 0))
        for piece in range(DH // chunk):
            start = (head * (DH // chunk) + piece) * step
            out_ref[start : start + chunk, :] = ahead[piece * chunk : (piece + 1) * chunk, :]
        gain_row = jnp.sum(gated_ref[:, at] * (attention * inverse), axis=0, keepdims=True)
        for block in range(head, members, heads):
            out_ref[block * step + chunk : (block + 1) * step, :] = gain_row


def early_grads_kernel(
    spans_ref, stats_ref, attention_ref, scaled_ref, gate_ref, grad_ref, q_ref, k_ref, v_ref,
    weights_ref, prefix_ref, early_ref, grad_q_ref, grad_gate_ref, local_k_ref, local_v_ref,
):
    rows, features = q_ref.shape
    inverse, _ = token_scales(stats_ref)
    for head in range(features // DH):
        at = cols(head)
        normed = attention_ref[:, at] * inverse
        rest = 1.0 - jax.nn.sigmoid(gate_ref[:, at].astype(wide))
        grad_gate_ref[:, at] = (scaled_ref[:, at] * normed * rest).astype(half)
        grad = grad_ref[:, at]
        square = decay_square(spans_ref[8 + head : 9 + head, :], rows)
        grad_scores = (dot_nt(grad, v_ref[:, at]) * square).astype(half)
        carried = dot_nt(twice(grad, 1), halves(prefix_ref[at, :], 1)) * (1.0 / DH)
        grad_q = dot(grad_scores, k_ref[:, at]) + early_ref[:, at] * carried
        grad_q_ref[:, at] = grad_q.astype(half)
        local_k_ref[:, at] = dot_tn(grad_scores, q_ref[:, at])
        local_v_ref[:, at] = dot_tn(weights_ref[:, at], grad)


def final_kernel(
    members, back_ref, k_ref, v_ref, local_k_ref, local_v_ref, late_ref, grad_k_ref, grad_v_ref, gain_ref,
    keys, values, gain, left,
):
    rows, features = k_ref.shape
    heads = features // DH
    copies = []

    def send(source, target):
        copy = pltpu.make_async_copy(source, target, left.at[len(copies)])
        copy.start()
        copies.append(copy)

    step = back_ref.shape[0] // members
    chunk = step - 1
    pieces = DH // chunk
    for head in range(heads):
        gain[:, cols(head)] = back_ref[head * step + chunk : (head + 1) * step, :]
    send(gain, gain_ref)
    for head in range(heads):
        at = cols(head)
        late = late_ref[:, at]
        starts = [block * step for block in range(head * pieces, (head + 1) * pieces)]
        suffix = jnp.concatenate([back_ref[start : start + chunk, :] for start in starts], axis=0)
        high = suffix.astype(half)
        low = (suffix - high.astype(wide)).astype(half)
        carried_k = dot_nt(twice(v_ref[:, at], 1), jnp.concatenate([high, low], axis=1))
        carried_v = dot(twice(k_ref[:, at], 1), jnp.concatenate([high, low], axis=0))
        keys[:, at] = (local_k_ref[:, at] + late * carried_k).astype(half)
        send(keys.at[:, at], grad_k_ref.at[:, at])
        values[:, at] = (local_v_ref[:, at] + late * carried_v).astype(half)
        send(values.at[:, at], grad_v_ref.at[:, at])
    for copy in copies:
        copy.wait()


def call(kernel, name, shapes, *operands, place=pltpu.VMEM, out_place=pltpu.VMEM, scratch=(), flops=0, bytes_moved=0):
    out_shape = [jax.ShapeDtypeStruct(*shape) for shape in shapes]
    results = pl.pallas_call(
        kernel,
        out_shape=out_shape,
        in_specs=[pl.BlockSpec(memory_space=place)] * len(operands),
        out_specs=[pl.BlockSpec(memory_space=out_place)] * len(out_shape),
        scratch_shapes=list(scratch),
        compiler_params=pltpu.CompilerParams(vmem_limit_bytes=24 * 1024 * 1024),
        cost_estimate=pl.CostEstimate(flops=flops, bytes_accessed=bytes_moved, transcendentals=0),
        name=name,
    )(*operands)
    return results if len(out_shape) > 1 else results[0]


def body(queries, key_rows, value_rows, gate_in, grad_out, decay_ints, norm_gain):
    rows, features = queries.shape
    members = lax.axis_size("ctx")
    head_members = lax.axis_size("head")
    chunk = features // members
    step = chunk + 1
    area = rows * features
    flat = ((features, DH), wide)
    long = ((members * step, DH), wide)
    block_wide = ((rows, features), wide)
    block_half = ((rows, features), half)

    def across(array, width):
        shape = (members, width, DH) if width % 8 == 0 else (members, width, 1, DH)
        return swap(array.reshape(shape), "ctx").reshape(members * width, DH)

    def sized(kernel):
        return functools.partial(kernel, members)

    summary, spans = call(
        sized(summary_kernel),
        "summary",
        [flat, ((16, DH), wide)],
        *[pltpu.with_memory_space_constraint(a, pltpu.HBM) for a in (decay_ints, key_rows, value_rows)],
        place=pltpu.HBM,
        scratch=[
            pltpu.SMEM(decay_ints.shape, jnp.int32),
            pltpu.VMEM((rows, features), half),
            pltpu.VMEM((rows, features), half),
            pltpu.VMEM((rows, features), wide),
            pltpu.SemaphoreType.DMA((3,)),
        ],
    )
    there = across(summary, chunk)
    local, weights, gated, scaled, queries_t, early, late = call(
        local_kernel,
        "local_attention",
        [block_wide, block_half, block_wide, block_wide, ((features, rows), half), block_wide, block_wide],
        spans, queries, key_rows, value_rows, gate_in, grad_out, norm_gain.reshape(1, features),
        flops=8 * area * DH, bytes_moved=28 * area,
    )
    prefix = across(call(sized(forward_kernel), "forward_scan", [flat], spans, there), chunk)
    attention, stats = call(
        attend_kernel,
        "attend",
        [block_wide, ((head_members, 8, rows), wide)],
        queries, prefix, local, scaled, early,
    )
    stats = swap(stats, "head")
    grad, message = call(
        sized(ahead_kernel),
        "ahead",
        [block_half, long],
        stats, attention, gated, scaled, queries_t, early,
    )
    there = across(message, step)
    grad_q, grad_gate, local_k, local_v = call(
        early_grads_kernel,
        "early_grads",
        [block_half, block_half, block_wide, block_wide],
        spans, stats, attention, scaled, gate_in, grad, queries, key_rows, value_rows,
        weights, prefix, early,
        flops=20 * area * DH, bytes_moved=28 * area,
    )
    back = across(call(sized(backward_kernel), "backward_scan", [long], spans, there), step)
    grad_k, grad_v, grad_gain = call(
        sized(final_kernel),
        "final",
        [block_half, block_half, ((1, features), wide)],
        back, key_rows, value_rows, local_k, local_v, late,
        out_place=pltpu.HBM,
        scratch=[
            pltpu.VMEM((rows, features), half),
            pltpu.VMEM((rows, features), half),
            pltpu.VMEM((1, features), wide),
            pltpu.SemaphoreType.DMA((2 * features // DH + 1,)),
        ],
    )
    return grad_q, grad_k, grad_v, grad_gate, grad_gain.reshape(features)


def solution(mesh):
    placed = (
        P("ctx", "head"),
        P("ctx", "head"),
        P("ctx", "head"),
        P("ctx", "head"),
        P("ctx", "head"),
        P("head"),
        P("head"),
    )
    return jax.shard_map(
        body,
        mesh=mesh,
        in_specs=placed,
        out_specs=(
            P("ctx", "head"),
            P("ctx", "head"),
            P("ctx", "head"),
            P("ctx", "head"),
            P("head"),
        ),
        check_vma=False,
    )
```

```python
import functools

import jax
import jax.numpy as jnp
from jax import lax
from jax.experimental import pallas as pl
from jax.experimental.pallas import tpu as pltpu
from jax.sharding import PartitionSpec as P

DH = 128
HD = 8192


rate_unit = 2.0 ** (-20)
norm_eps = 1e-06
wide = jnp.float32
half = jnp.bfloat16


def swap(array, axis):
    return lax.all_to_all(array, axis, 0, 0)


def halves(array, axis):
    high = array.astype(half)
    low = (array - high.astype(wide)).astype(half)
    return jnp.concatenate([high, low], axis=axis)


def twice(array, axis):
    return jnp.concatenate([array, array], axis=axis)


def dot(left, right):
    return jnp.dot(left, right, preferred_element_type=wide)


def dot_nt(left, right):
    return lax.dot_general(left, right, (((1,), (1,)), ((), ())), preferred_element_type=wide)


def dot_tn(left, right):
    return lax.dot_general(left, right, (((0,), (0,)), ((), ())), preferred_element_type=wide)


def rate_of(ints_ref, head):
    return ints_ref[head].astype(wide) * rate_unit


def decay_column(rate, rows, late):
    place = lax.broadcasted_iota(jnp.int32, (rows, DH), 0).astype(wide)
    return jnp.exp(-rate * ((rows - 1.0 - place) if late else (place + 1.0)))


def decay_square(rate, rows):
    later = lax.broadcasted_iota(jnp.int32, (rows, rows), 0)
    sooner = lax.broadcasted_iota(jnp.int32, (rows, rows), 1)
    gap = (later - sooner).astype(wide)
    return jnp.where(gap >= 0.0, jnp.exp(-rate * jnp.maximum(gap, 0.0)), 0.0) * (1.0 / DH)


def cols(head):
    return slice(head * DH, (head + 1) * DH)


def summary_kernel(members, ints_ref, k_ref, v_ref, out_ref, spans_ref, ints, keys, values, late, arrived):
    rows, features = k_ref.shape
    heads = features // DH
    copies = [
        pltpu.make_async_copy(source, target, arrived.at[number])
        for number, (source, target) in enumerate(((ints_ref, ints), (k_ref, keys), (v_ref, values)))
    ]
    for copy in copies:
        copy.start()
    copies[0].wait()
    owned = lax.axis_index("ctx") * (features // members) // DH
    power = lax.broadcasted_iota(jnp.int32, (8, DH), 0).astype(wide) + 1.0
    spans_ref[0:8, :] = jnp.exp(-(rate_of(ints, owned) * rows) * power)
    for head in range(heads):
        spans_ref[8 + head : 9 + head, :] = jnp.full((1, DH), rate_of(ints, head), wide)
        late[:, cols(head)] = decay_column(rate_of(ints, head), rows, True)
    copies[1].wait()
    copies[2].wait()
    for head in range(heads):
        weighted = late[:, cols(head)] * values[:, cols(head)].astype(wide)
        out_ref[cols(head), :] = dot(twice(keys[:, cols(head)].T, 1), halves(weighted, 0))


def scan_blocks(order, span, leap, take, put, zero):
    chains = [order[at : at + 8] for at in range(0, len(order), 8)]
    totals = [take(chain[0]) for chain in chains]
    for turn in range(1, 8):
        blocks = [take(chain[turn]) for chain in chains]
        totals = [span * total + block for total, block in zip(totals, blocks)]
    states = [zero]
    for total in totals[:-1]:
        states.append(leap * states[-1] + total)
    for turn in range(8):
        blocks = [take(chain[turn]) for chain in chains]
        for chain, state in zip(chains, states):
            put(chain[turn], state)
        states = [span * state + block for state, block in zip(states, blocks)]


def forward_kernel(members, spans_ref, in_ref, out_ref):
    chunk = in_ref.shape[0] // members

    def take(block):
        return in_ref[block * chunk : (block + 1) * chunk, :]

    def put(block, state):
        out_ref[block * chunk : (block + 1) * chunk, :] = state

    order = list(range(members))
    scan_blocks(order, spans_ref[0:1, :], spans_ref[7:8, :], take, put, jnp.zeros((chunk, DH), wide))


def backward_kernel(members, spans_ref, in_ref, out_ref):
    step = in_ref.shape[0] // members
    chunk = step - 1

    def take(block):
        return in_ref[block * step : block * step + chunk, :]

    def put(block, state):
        out_ref[block * step : block * step + chunk, :] = state

    order = list(reversed(range(members)))
    scan_blocks(order, spans_ref[0:1, :], spans_ref[7:8, :], take, put, jnp.zeros((chunk, DH), wide))
    gains = [in_ref[block * step + chunk : (block + 1) * step, :] for block in range(members)]
    while len(gains) > 1:
        gains = [gains[at] + gains[at + 1] for at in range(0, len(gains), 2)]
    for block in range(members):
        out_ref[block * step + chunk : (block + 1) * step, :] = gains[0]


def attend_kernel(
    spans_ref, q_ref, k_ref, v_ref, gate_ref, grad_ref, gain_ref, prefix_ref,
    attention_ref, stats_ref, weights_ref, gated_ref, scaled_ref, early_ref,
):
    rows, features = q_ref.shape
    squares = jnp.zeros((rows, DH), wide)
    crossed = jnp.zeros((rows, DH), wide)
    for head in range(features // DH):
        at = cols(head)
        rate = spans_ref[8 + head : 9 + head, :]
        queries = q_ref[:, at]
        weights = (dot_nt(queries, k_ref[:, at]) * decay_square(rate, rows)).astype(half)
        weights_ref[:, at] = weights
        gated = grad_ref[:, at].astype(wide) * jax.nn.sigmoid(gate_ref[:, at].astype(wide))
        gated_ref[:, at] = gated
        scaled = gated * gain_ref[:, at]
        scaled_ref[:, at] = scaled
        early = decay_column(rate, rows, False)
        early_ref[:, at] = early
        carried = dot(twice(queries, 1), halves(prefix_ref[at, :], 0)) * (1.0 / DH)
        attention = dot(weights, v_ref[:, at]) + early * carried
        attention_ref[:, at] = attention
        squares = squares + attention * attention
        crossed = crossed + scaled * attention
    squares = jnp.sum(squares.T, axis=0, keepdims=True)
    crossed = jnp.sum(crossed.T, axis=0, keepdims=True)
    line = lax.broadcasted_iota(jnp.int32, (8, DH), 0)
    pair = jnp.where(line == 0, squares, jnp.where(line == 1, crossed, 0.0))
    for member in range(stats_ref.shape[0]):
        stats_ref[member] = pair


def token_scales(stats_ref):
    total = stats_ref[0]
    for member in range(1, stats_ref.shape[0]):
        total = total + stats_ref[member]
    inverse = lax.rsqrt(total[0:1] * (1.0 / HD) + norm_eps)
    pull = inverse * inverse * inverse * total[1:2] * (1.0 / HD)
    line = lax.broadcasted_iota(jnp.int32, (8, DH), 0)
    columns = jnp.where(line == 0, inverse, jnp.where(line == 1, pull, 0.0)).T
    return columns[:, 0:1], columns[:, 1:2]


def ahead_kernel(
    members, stats_ref, attention_ref, gated_ref, scaled_ref, q_ref, early_ref, grad_ref, out_ref
):
    rows, features = attention_ref.shape
    heads = features // DH
    step = out_ref.shape[0] // members
    chunk = step - 1
    inverse, pull = token_scales(stats_ref)
    for head in range(heads):
        at = cols(head)
        attention = attention_ref[:, at]
        grad = (inverse * scaled_ref[:, at] - pull * attention).astype(half)
        grad_ref[:, at] = grad
        ahead = dot(twice(q_ref[:, at].T, 1), halves(early_ref[:, at] * grad.astype(wide), 0))
        for piece in range(DH // chunk):
            start = (head * (DH // chunk) + piece) * step
            out_ref[start : start + chunk, :] = ahead[piece * chunk : (piece + 1) * chunk, :]
        gain_row = jnp.sum(gated_ref[:, at] * (attention * inverse), axis=0, keepdims=True)
        for block in range(head, members, heads):
            out_ref[block * step + chunk : (block + 1) * step, :] = gain_row


def early_grads_kernel(
    spans_ref, stats_ref, attention_ref, scaled_ref, gate_ref, grad_ref, q_ref, k_ref, v_ref,
    weights_ref, prefix_ref, early_ref, grad_q_ref, grad_gate_ref, local_k_ref, local_v_ref, late_ref,
):
    rows, features = q_ref.shape
    inverse, _ = token_scales(stats_ref)
    for head in range(features // DH):
        at = cols(head)
        normed = attention_ref[:, at] * inverse
        rest = 1.0 - jax.nn.sigmoid(gate_ref[:, at].astype(wide))
        grad_gate_ref[:, at] = (scaled_ref[:, at] * normed * rest).astype(half)
        grad = grad_ref[:, at]
        rate = spans_ref[8 + head : 9 + head, :]
        late_ref[:, at] = decay_column(rate, rows, True) * (1.0 / DH)
        square = decay_square(rate, rows)
        grad_scores = (dot_nt(grad, v_ref[:, at]) * square).astype(half)
        carried = dot_nt(twice(grad, 1), halves(prefix_ref[at, :], 1)) * (1.0 / DH)
        grad_q = dot(grad_scores, k_ref[:, at]) + early_ref[:, at] * carried
        grad_q_ref[:, at] = grad_q.astype(half)
        local_k_ref[:, at] = dot_tn(grad_scores, q_ref[:, at])
        local_v_ref[:, at] = dot_tn(weights_ref[:, at], grad)


def final_kernel(
    members, back_ref, k_ref, v_ref, local_k_ref, local_v_ref, late_ref, grad_k_ref, grad_v_ref, gain_ref,
    keys, values, gain, left,
):
    rows, features = k_ref.shape
    heads = features // DH
    copies = []

    def send(source, target):
        copy = pltpu.make_async_copy(source, target, left.at[len(copies)])
        copy.start()
        copies.append(copy)

    step = back_ref.shape[0] // members
    chunk = step - 1
    pieces = DH // chunk
    for head in range(heads):
        gain[:, cols(head)] = back_ref[head * step + chunk : (head + 1) * step, :]
    send(gain, gain_ref)
    for head in range(heads):
        at = cols(head)
        late = late_ref[:, at]
        starts = [block * step for block in range(head * pieces, (head + 1) * pieces)]
        suffix = jnp.concatenate([back_ref[start : start + chunk, :] for start in starts], axis=0)
        high = suffix.astype(half)
        low = (suffix - high.astype(wide)).astype(half)
        carried_k = dot_nt(twice(v_ref[:, at], 1), jnp.concatenate([high, low], axis=1))
        carried_v = dot(twice(k_ref[:, at], 1), jnp.concatenate([high, low], axis=0))
        keys[:, at] = (local_k_ref[:, at] + late * carried_k).astype(half)
        send(keys.at[:, at], grad_k_ref.at[:, at])
        values[:, at] = (local_v_ref[:, at] + late * carried_v).astype(half)
        send(values.at[:, at], grad_v_ref.at[:, at])
    for copy in copies:
        copy.wait()


def call(kernel, name, shapes, *operands, place=pltpu.VMEM, out_place=pltpu.VMEM, scratch=(), flops=0, bytes_moved=0):
    out_shape = [jax.ShapeDtypeStruct(*shape) for shape in shapes]
    results = pl.pallas_call(
        kernel,
        out_shape=out_shape,
        in_specs=[pl.BlockSpec(memory_space=place)] * len(operands),
        out_specs=[pl.BlockSpec(memory_space=out_place)] * len(out_shape),
        scratch_shapes=list(scratch),
        compiler_params=pltpu.CompilerParams(vmem_limit_bytes=24 * 1024 * 1024),
        cost_estimate=pl.CostEstimate(flops=flops, bytes_accessed=bytes_moved, transcendentals=0),
        name=name,
    )(*operands)
    return results if len(out_shape) > 1 else results[0]


def body(queries, key_rows, value_rows, gate_in, grad_out, decay_ints, norm_gain):
    rows, features = queries.shape
    members = lax.axis_size("ctx")
    head_members = lax.axis_size("head")
    chunk = features // members
    step = chunk + 1
    area = rows * features
    flat = ((features, DH), wide)
    long = ((members * step, DH), wide)
    block_wide = ((rows, features), wide)
    block_half = ((rows, features), half)

    def across(array, width):
        shape = (members, width, DH) if width % 8 == 0 else (members, width, 1, DH)
        return swap(array.reshape(shape), "ctx").reshape(members * width, DH)

    def sized(kernel):
        return functools.partial(kernel, members)

    summary, spans = call(
        sized(summary_kernel),
        "summary",
        [flat, ((16, DH), wide)],
        *[pltpu.with_memory_space_constraint(a, pltpu.HBM) for a in (decay_ints, key_rows, value_rows)],
        place=pltpu.HBM,
        scratch=[
            pltpu.SMEM(decay_ints.shape, jnp.int32),
            pltpu.VMEM((rows, features), half),
            pltpu.VMEM((rows, features), half),
            pltpu.VMEM((rows, features), wide),
            pltpu.SemaphoreType.DMA((3,)),
        ],
    )
    there = across(summary, chunk)
    prefix = across(call(sized(forward_kernel), "forward_scan", [flat], spans, there), chunk)
    attention, stats, weights, gated, scaled, early = call(
        attend_kernel,
        "attend",
        [block_wide, ((head_members, 8, rows), wide), block_half, block_wide, block_wide, block_wide],
        spans, queries, key_rows, value_rows, gate_in, grad_out, norm_gain.reshape(1, features), prefix,
    )
    stats = swap(stats, "head")
    grad, message = call(
        sized(ahead_kernel),
        "ahead",
        [block_half, long],
        stats, attention, gated, scaled, queries, early,
    )
    there = across(message, step)
    grad_q, grad_gate, local_k, local_v, late = call(
        early_grads_kernel,
        "early_grads",
        [block_half, block_half, block_wide, block_wide, block_wide],
        spans, stats, attention, scaled, gate_in, grad, queries, key_rows, value_rows,
        weights, prefix, early,
        flops=20 * area * DH, bytes_moved=28 * area,
    )
    back = across(call(sized(backward_kernel), "backward_scan", [long], spans, there), step)
    grad_k, grad_v, grad_gain = call(
        sized(final_kernel),
        "final",
        [block_half, block_half, ((1, features), wide)],
        back, key_rows, value_rows, local_k, local_v, late,
        out_place=pltpu.HBM,
        scratch=[
            pltpu.VMEM((rows, features), half),
            pltpu.VMEM((rows, features), half),
            pltpu.VMEM((1, features), wide),
            pltpu.SemaphoreType.DMA((2 * features // DH + 1,)),
        ],
    )
    return grad_q, grad_k, grad_v, grad_gate, grad_gain.reshape(features)


def solution(mesh):
    placed = (
        P("ctx", "head"),
        P("ctx", "head"),
        P("ctx", "head"),
        P("ctx", "head"),
        P("ctx", "head"),
        P("head"),
        P("head"),
    )
    return jax.shard_map(
        body,
        mesh=mesh,
        in_specs=placed,
        out_specs=(
            P("ctx", "head"),
            P("ctx", "head"),
            P("ctx", "head"),
            P("ctx", "head"),
            P("head"),
        ),
        check_vma=False,
    )
```

```python
import functools

import jax
import jax.numpy as jnp
from jax import lax
from jax.experimental import pallas as pl
from jax.experimental.pallas import tpu as pltpu
from jax.sharding import PartitionSpec as P

DH = 128
HD = 8192


rate_unit = 2.0 ** (-20)
norm_eps = 1e-06
wide = jnp.float32
half = jnp.bfloat16


def swap(array, axis):
    return lax.all_to_all(array, axis, 0, 0)


def halves(array, axis):
    high = array.astype(half)
    low = (array - high.astype(wide)).astype(half)
    return jnp.concatenate([high, low], axis=axis)


def twice(array, axis):
    return jnp.concatenate([array, array], axis=axis)


def dot(left, right):
    return jnp.dot(left, right, preferred_element_type=wide)


def dot_nt(left, right):
    return lax.dot_general(left, right, (((1,), (1,)), ((), ())), preferred_element_type=wide)


def dot_tn(left, right):
    return lax.dot_general(left, right, (((0,), (0,)), ((), ())), preferred_element_type=wide)


def rate_of(ints_ref, head):
    return ints_ref[head].astype(wide) * rate_unit


def decay_column(rate, rows, late):
    place = lax.broadcasted_iota(jnp.int32, (rows, DH), 0).astype(wide)
    return jnp.exp(-rate * ((rows - 1.0 - place) if late else (place + 1.0)))


def decay_square(rate, rows):
    later = lax.broadcasted_iota(jnp.int32, (rows, rows), 0)
    sooner = lax.broadcasted_iota(jnp.int32, (rows, rows), 1)
    gap = (later - sooner).astype(wide)
    return jnp.where(gap >= 0.0, jnp.exp(-rate * jnp.maximum(gap, 0.0)), 0.0) * (1.0 / DH)


def cols(head):
    return slice(head * DH, (head + 1) * DH)


def summary_kernel(
    members, ints_ref, k_ref, v_ref, gain_ref, out_ref, spans_ref, gain_out_ref, ints, keys, values, late, arrived
):
    rows, features = k_ref.shape
    heads = features // DH
    copies = [
        pltpu.make_async_copy(source, target, arrived.at[number])
        for number, (source, target) in enumerate(
            ((ints_ref, ints), (k_ref, keys), (v_ref, values), (gain_ref, gain_out_ref))
        )
    ]
    for copy in copies:
        copy.start()
    copies[0].wait()
    owned = lax.axis_index("ctx") * (features // members) // DH
    power = lax.broadcasted_iota(jnp.int32, (8, DH), 0).astype(wide) + 1.0
    spans_ref[0:8, :] = jnp.exp(-(rate_of(ints, owned) * rows) * power)
    for head in range(heads):
        spans_ref[8 + head : 9 + head, :] = jnp.full((1, DH), rate_of(ints, head), wide)
        late[:, cols(head)] = decay_column(rate_of(ints, head), rows, True)
    copies[1].wait()
    copies[2].wait()
    for head in range(heads):
        weighted = late[:, cols(head)] * values[:, cols(head)].astype(wide)
        out_ref[cols(head), :] = dot(twice(keys[:, cols(head)].T, 1), halves(weighted, 0))
    copies[3].wait()


def scan_blocks(order, span, leap, take, put, zero):
    chains = [order[at : at + 8] for at in range(0, len(order), 8)]
    totals = [take(chain[0]) for chain in chains]
    for turn in range(1, 8):
        blocks = [take(chain[turn]) for chain in chains]
        totals = [span * total + block for total, block in zip(totals, blocks)]
    states = [zero]
    for total in totals[:-1]:
        states.append(leap * states[-1] + total)
    for turn in range(8):
        blocks = [take(chain[turn]) for chain in chains]
        for chain, state in zip(chains, states):
            put(chain[turn], state)
        states = [span * state + block for state, block in zip(states, blocks)]


def forward_kernel(members, spans_ref, in_ref, out_ref):
    chunk = in_ref.shape[0] // members

    def take(block):
        return in_ref[block * chunk : (block + 1) * chunk, :]

    def put(block, state):
        out_ref[block * chunk : (block + 1) * chunk, :] = state

    order = list(range(members))
    scan_blocks(order, spans_ref[0:1, :], spans_ref[7:8, :], take, put, jnp.zeros((chunk, DH), wide))


def backward_kernel(members, spans_ref, in_ref, out_ref):
    step = in_ref.shape[0] // members
    chunk = step - 1

    def take(block):
        return in_ref[block * step : block * step + chunk, :]

    def put(block, state):
        out_ref[block * step : block * step + chunk, :] = state

    order = list(reversed(range(members)))
    scan_blocks(order, spans_ref[0:1, :], spans_ref[7:8, :], take, put, jnp.zeros((chunk, DH), wide))
    gains = [in_ref[block * step + chunk : (block + 1) * step, :] for block in range(members)]
    while len(gains) > 1:
        gains = [gains[at] + gains[at + 1] for at in range(0, len(gains), 2)]
    for block in range(members):
        out_ref[block * step + chunk : (block + 1) * step, :] = gains[0]


def attend_kernel(
    spans_ref, q_ref, k_ref, v_ref, gate_ref, grad_ref, gain_ref, prefix_ref,
    attention_ref, stats_ref, weights_ref, gated_ref, scaled_ref, early_ref,
):
    rows, features = q_ref.shape
    squares = jnp.zeros((rows, DH), wide)
    crossed = jnp.zeros((rows, DH), wide)
    for head in range(features // DH):
        at = cols(head)
        rate = spans_ref[8 + head : 9 + head, :]
        queries = q_ref[:, at]
        weights = (dot_nt(queries, k_ref[:, at]) * decay_square(rate, rows)).astype(half)
        weights_ref[:, at] = weights
        gated = grad_ref[:, at].astype(wide) * jax.nn.sigmoid(gate_ref[:, at].astype(wide))
        gated_ref[:, at] = gated
        scaled = gated * gain_ref[:, at]
        scaled_ref[:, at] = scaled
        early = decay_column(rate, rows, False)
        early_ref[:, at] = early
        carried = dot(twice(queries, 1), halves(prefix_ref[at, :], 0)) * (1.0 / DH)
        attention = dot(weights, v_ref[:, at]) + early * carried
        attention_ref[:, at] = attention
        squares = squares + attention * attention
        crossed = crossed + scaled * attention
    squares = jnp.sum(squares.T, axis=0, keepdims=True)
    crossed = jnp.sum(crossed.T, axis=0, keepdims=True)
    line = lax.broadcasted_iota(jnp.int32, (8, DH), 0)
    pair = jnp.where(line == 0, squares, jnp.where(line == 1, crossed, 0.0))
    for member in range(stats_ref.shape[0]):
        stats_ref[member] = pair


def token_scales(stats_ref):
    total = stats_ref[0]
    for member in range(1, stats_ref.shape[0]):
        total = total + stats_ref[member]
    inverse = lax.rsqrt(total[0:1] * (1.0 / HD) + norm_eps)
    pull = inverse * inverse * inverse * total[1:2] * (1.0 / HD)
    line = lax.broadcasted_iota(jnp.int32, (8, DH), 0)
    columns = jnp.where(line == 0, inverse, jnp.where(line == 1, pull, 0.0)).T
    return columns[:, 0:1], columns[:, 1:2]


def ahead_kernel(
    members, stats_ref, attention_ref, gated_ref, scaled_ref, q_ref, early_ref, grad_ref, out_ref
):
    rows, features = attention_ref.shape
    heads = features // DH
    step = out_ref.shape[0] // members
    chunk = step - 1
    inverse, pull = token_scales(stats_ref)
    for head in range(heads):
        at = cols(head)
        attention = attention_ref[:, at]
        grad = (inverse * scaled_ref[:, at] - pull * attention).astype(half)
        grad_ref[:, at] = grad
        ahead = dot(twice(q_ref[:, at].T, 1), halves(early_ref[:, at] * grad.astype(wide), 0))
        for piece in range(DH // chunk):
            start = (head * (DH // chunk) + piece) * step
            out_ref[start : start + chunk, :] = ahead[piece * chunk : (piece + 1) * chunk, :]
        gain_row = jnp.sum(gated_ref[:, at] * (attention * inverse), axis=0, keepdims=True)
        for block in range(head, members, heads):
            out_ref[block * step + chunk : (block + 1) * step, :] = gain_row


def early_grads_kernel(
    spans_ref, stats_ref, attention_ref, scaled_ref, gate_ref, grad_ref, q_ref, k_ref, v_ref,
    weights_ref, prefix_ref, early_ref, grad_q_ref, grad_gate_ref, local_k_ref, local_v_ref, late_ref,
):
    rows, features = q_ref.shape
    inverse, _ = token_scales(stats_ref)
    for head in range(features // DH):
        at = cols(head)
        normed = attention_ref[:, at] * inverse
        rest = 1.0 - jax.nn.sigmoid(gate_ref[:, at].astype(wide))
        grad_gate_ref[:, at] = (scaled_ref[:, at] * normed * rest).astype(half)
        grad = grad_ref[:, at]
        rate = spans_ref[8 + head : 9 + head, :]
        late_ref[:, at] = decay_column(rate, rows, True) * (1.0 / DH)
        square = decay_square(rate, rows)
        grad_scores = (dot_nt(grad, v_ref[:, at]) * square).astype(half)
        carried = dot_nt(twice(grad, 1), halves(prefix_ref[at, :], 1)) * (1.0 / DH)
        grad_q = dot(grad_scores, k_ref[:, at]) + early_ref[:, at] * carried
        grad_q_ref[:, at] = grad_q.astype(half)
        local_k_ref[:, at] = dot_tn(grad_scores, q_ref[:, at])
        local_v_ref[:, at] = dot_tn(weights_ref[:, at], grad)


def final_kernel(
    members, back_ref, k_ref, v_ref, local_k_ref, local_v_ref, late_ref, grad_k_ref, grad_v_ref, gain_ref,
    keys, values, gain, left,
):
    rows, features = k_ref.shape
    heads = features // DH
    copies = []

    def send(source, target):
        copy = pltpu.make_async_copy(source, target, left.at[len(copies)])
        copy.start()
        copies.append(copy)

    step = back_ref.shape[0] // members
    chunk = step - 1
    pieces = DH // chunk
    for head in range(heads):
        gain[:, cols(head)] = back_ref[head * step + chunk : (head + 1) * step, :]
    send(gain, gain_ref)
    for head in range(heads):
        at = cols(head)
        late = late_ref[:, at]
        starts = [block * step for block in range(head * pieces, (head + 1) * pieces)]
        suffix = jnp.concatenate([back_ref[start : start + chunk, :] for start in starts], axis=0)
        high = suffix.astype(half)
        low = (suffix - high.astype(wide)).astype(half)
        carried_k = dot_nt(twice(v_ref[:, at], 1), jnp.concatenate([high, low], axis=1))
        carried_v = dot(twice(k_ref[:, at], 1), jnp.concatenate([high, low], axis=0))
        keys[:, at] = (local_k_ref[:, at] + late * carried_k).astype(half)
        send(keys.at[:, at], grad_k_ref.at[:, at])
        values[:, at] = (local_v_ref[:, at] + late * carried_v).astype(half)
        send(values.at[:, at], grad_v_ref.at[:, at])
    for copy in copies:
        copy.wait()


def call(kernel, name, shapes, *operands, place=pltpu.VMEM, out_place=pltpu.VMEM, scratch=(), flops=0, bytes_moved=0):
    out_shape = [jax.ShapeDtypeStruct(*shape) for shape in shapes]
    results = pl.pallas_call(
        kernel,
        out_shape=out_shape,
        in_specs=[pl.BlockSpec(memory_space=place)] * len(operands),
        out_specs=[pl.BlockSpec(memory_space=out_place)] * len(out_shape),
        scratch_shapes=list(scratch),
        compiler_params=pltpu.CompilerParams(vmem_limit_bytes=24 * 1024 * 1024),
        cost_estimate=pl.CostEstimate(flops=flops, bytes_accessed=bytes_moved, transcendentals=0),
        name=name,
    )(*operands)
    return results if len(out_shape) > 1 else results[0]


def body(queries, key_rows, value_rows, gate_in, grad_out, decay_ints, norm_gain):
    rows, features = queries.shape
    members = lax.axis_size("ctx")
    head_members = lax.axis_size("head")
    chunk = features // members
    step = chunk + 1
    area = rows * features
    flat = ((features, DH), wide)
    long = ((members * step, DH), wide)
    block_wide = ((rows, features), wide)
    block_half = ((rows, features), half)

    def across(array, width):
        shape = (members, width, DH) if width % 8 == 0 else (members, width, 1, DH)
        return swap(array.reshape(shape), "ctx").reshape(members * width, DH)

    def sized(kernel):
        return functools.partial(kernel, members)

    given = (decay_ints, key_rows, value_rows, norm_gain.reshape(1, features))
    summary, spans, gain = call(
        sized(summary_kernel),
        "summary",
        [flat, ((16, DH), wide), ((1, features), wide)],
        *[pltpu.with_memory_space_constraint(a, pltpu.HBM) for a in given],
        place=pltpu.HBM,
        scratch=[
            pltpu.SMEM(decay_ints.shape, jnp.int32),
            pltpu.VMEM((rows, features), half),
            pltpu.VMEM((rows, features), half),
            pltpu.VMEM((rows, features), wide),
            pltpu.SemaphoreType.DMA((4,)),
        ],
    )
    there = across(summary, chunk)
    prefix = across(call(sized(forward_kernel), "forward_scan", [flat], spans, there), chunk)
    attention, stats, weights, gated, scaled, early = call(
        attend_kernel,
        "attend",
        [block_wide, ((head_members, 8, rows), wide), block_half, block_wide, block_wide, block_wide],
        spans, queries, key_rows, value_rows, gate_in, grad_out, gain, prefix,
    )
    stats = swap(stats, "head")
    grad, message = call(
        sized(ahead_kernel),
        "ahead",
        [block_half, long],
        stats, attention, gated, scaled, queries, early,
    )
    there = across(message, step)
    grad_q, grad_gate, local_k, local_v, late = call(
        early_grads_kernel,
        "early_grads",
        [block_half, block_half, block_wide, block_wide, block_wide],
        spans, stats, attention, scaled, gate_in, grad, queries, key_rows, value_rows,
        weights, prefix, early,
        flops=20 * area * DH, bytes_moved=28 * area,
    )
    back = across(call(sized(backward_kernel), "backward_scan", [long], spans, there), step)
    grad_k, grad_v, grad_gain = call(
        sized(final_kernel),
        "final",
        [block_half, block_half, ((1, features), wide)],
        back, key_rows, value_rows, local_k, local_v, late,
        out_place=pltpu.HBM,
        scratch=[
            pltpu.VMEM((rows, features), half),
            pltpu.VMEM((rows, features), half),
            pltpu.VMEM((1, features), wide),
            pltpu.SemaphoreType.DMA((2 * features // DH + 1,)),
        ],
    )
    return grad_q, grad_k, grad_v, grad_gate, grad_gain.reshape(features)


def solution(mesh):
    placed = (
        P("ctx", "head"),
        P("ctx", "head"),
        P("ctx", "head"),
        P("ctx", "head"),
        P("ctx", "head"),
        P("head"),
        P("head"),
    )
    return jax.shard_map(
        body,
        mesh=mesh,
        in_specs=placed,
        out_specs=(
            P("ctx", "head"),
            P("ctx", "head"),
            P("ctx", "head"),
            P("ctx", "head"),
            P("head"),
        ),
        check_vma=False,
    )
```

```python
import functools

import jax
import jax.numpy as jnp
from jax import lax
from jax.experimental import pallas as pl
from jax.experimental.pallas import tpu as pltpu
from jax.sharding import PartitionSpec as P

DH = 128
HD = 8192


rate_unit = 2.0 ** (-20)
norm_eps = 1e-06
first_place = {"ctx": 36, "head": 14}
wide = jnp.float32
half = jnp.bfloat16


def swap(array, axis):
    size, first = lax.axis_size(axis), first_place[axis]
    groups = [[(first + slot) % size for slot in range(size)]]
    return lax.all_to_all(array, axis, 0, 0, axis_index_groups=groups)


def ctx_slots(members):
    return [(block - first_place["ctx"]) % members for block in range(members)]


def halves(array, axis):
    high = array.astype(half)
    low = (array - high.astype(wide)).astype(half)
    return jnp.concatenate([high, low], axis=axis)


def twice(array, axis):
    return jnp.concatenate([array, array], axis=axis)


def dot(left, right):
    return jnp.dot(left, right, preferred_element_type=wide)


def dot_nt(left, right):
    return lax.dot_general(left, right, (((1,), (1,)), ((), ())), preferred_element_type=wide)


def dot_tn(left, right):
    return lax.dot_general(left, right, (((0,), (0,)), ((), ())), preferred_element_type=wide)


def rate_of(ints_ref, head):
    return ints_ref[head].astype(wide) * rate_unit


def decay_column(rate, rows, late):
    place = lax.broadcasted_iota(jnp.int32, (rows, DH), 0).astype(wide)
    return jnp.exp(-rate * ((rows - 1.0 - place) if late else (place + 1.0)))


def decay_square(rate, rows):
    later = lax.broadcasted_iota(jnp.int32, (rows, rows), 0)
    sooner = lax.broadcasted_iota(jnp.int32, (rows, rows), 1)
    gap = (later - sooner).astype(wide)
    return jnp.where(gap >= 0.0, jnp.exp(-rate * jnp.maximum(gap, 0.0)), 0.0) * (1.0 / DH)


def cols(head):
    return slice(head * DH, (head + 1) * DH)


def summary_kernel(
    members, ints_ref, k_ref, v_ref, gain_ref, out_ref, spans_ref, gain_out_ref, ints, keys, values, late, arrived
):
    rows, features = k_ref.shape
    heads = features // DH
    copies = [
        pltpu.make_async_copy(source, target, arrived.at[number])
        for number, (source, target) in enumerate(
            ((ints_ref, ints), (k_ref, keys), (v_ref, values), (gain_ref, gain_out_ref))
        )
    ]
    for copy in copies:
        copy.start()
    copies[0].wait()
    slot = (lax.axis_index("ctx") + (members - first_place["ctx"])) % members
    owned = slot * (features // members) // DH
    power = lax.broadcasted_iota(jnp.int32, (8, DH), 0).astype(wide) + 1.0
    spans_ref[0:8, :] = jnp.exp(-(rate_of(ints, owned) * rows) * power)
    for head in range(heads):
        spans_ref[8 + head : 9 + head, :] = jnp.full((1, DH), rate_of(ints, head), wide)
        late[:, cols(head)] = decay_column(rate_of(ints, head), rows, True)
    copies[1].wait()
    copies[2].wait()
    for head in range(heads):
        weighted = late[:, cols(head)] * values[:, cols(head)].astype(wide)
        out_ref[cols(head), :] = dot(twice(keys[:, cols(head)].T, 1), halves(weighted, 0))
    copies[3].wait()


def scan_blocks(order, span, leap, take, put, zero):
    chains = [order[at : at + 8] for at in range(0, len(order), 8)]
    totals = [take(chain[0]) for chain in chains]
    for turn in range(1, 8):
        blocks = [take(chain[turn]) for chain in chains]
        totals = [span * total + block for total, block in zip(totals, blocks)]
    states = [zero]
    for total in totals[:-1]:
        states.append(leap * states[-1] + total)
    for turn in range(8):
        blocks = [take(chain[turn]) for chain in chains]
        for chain, state in zip(chains, states):
            put(chain[turn], state)
        states = [span * state + block for state, block in zip(states, blocks)]


def forward_kernel(members, spans_ref, in_ref, out_ref):
    chunk = in_ref.shape[0] // members

    def take(block):
        return in_ref[block * chunk : (block + 1) * chunk, :]

    def put(block, state):
        out_ref[block * chunk : (block + 1) * chunk, :] = state

    order = ctx_slots(members)
    scan_blocks(order, spans_ref[0:1, :], spans_ref[7:8, :], take, put, jnp.zeros((chunk, DH), wide))


def backward_kernel(members, spans_ref, in_ref, out_ref):
    step = in_ref.shape[0] // members
    chunk = step - 1

    def take(block):
        return in_ref[block * step : block * step + chunk, :]

    def put(block, state):
        out_ref[block * step : block * step + chunk, :] = state

    order = list(reversed(ctx_slots(members)))
    scan_blocks(order, spans_ref[0:1, :], spans_ref[7:8, :], take, put, jnp.zeros((chunk, DH), wide))
    gains = [in_ref[block * step + chunk : (block + 1) * step, :] for block in range(members)]
    while len(gains) > 1:
        gains = [gains[at] + gains[at + 1] for at in range(0, len(gains), 2)]
    for block in range(members):
        out_ref[block * step + chunk : (block + 1) * step, :] = gains[0]


def attend_kernel(
    spans_ref, q_ref, k_ref, v_ref, gate_ref, grad_ref, gain_ref, prefix_ref,
    attention_ref, stats_ref, weights_ref, gated_ref, scaled_ref, early_ref,
):
    rows, features = q_ref.shape
    squares = jnp.zeros((rows, DH), wide)
    crossed = jnp.zeros((rows, DH), wide)
    for head in range(features // DH):
        at = cols(head)
        rate = spans_ref[8 + head : 9 + head, :]
        queries = q_ref[:, at]
        weights = (dot_nt(queries, k_ref[:, at]) * decay_square(rate, rows)).astype(half)
        weights_ref[:, at] = weights
        gated = grad_ref[:, at].astype(wide) * jax.nn.sigmoid(gate_ref[:, at].astype(wide))
        gated_ref[:, at] = gated
        scaled = gated * gain_ref[:, at]
        scaled_ref[:, at] = scaled
        early = decay_column(rate, rows, False)
        early_ref[:, at] = early
        carried = dot(twice(queries, 1), halves(prefix_ref[at, :], 0)) * (1.0 / DH)
        attention = dot(weights, v_ref[:, at]) + early * carried
        attention_ref[:, at] = attention
        squares = squares + attention * attention
        crossed = crossed + scaled * attention
    squares = jnp.sum(squares.T, axis=0, keepdims=True)
    crossed = jnp.sum(crossed.T, axis=0, keepdims=True)
    line = lax.broadcasted_iota(jnp.int32, (8, DH), 0)
    pair = jnp.where(line == 0, squares, jnp.where(line == 1, crossed, 0.0))
    for member in range(stats_ref.shape[0]):
        stats_ref[member] = pair


def token_scales(stats_ref):
    total = stats_ref[0]
    for member in range(1, stats_ref.shape[0]):
        total = total + stats_ref[member]
    inverse = lax.rsqrt(total[0:1] * (1.0 / HD) + norm_eps)
    pull = inverse * inverse * inverse * total[1:2] * (1.0 / HD)
    line = lax.broadcasted_iota(jnp.int32, (8, DH), 0)
    columns = jnp.where(line == 0, inverse, jnp.where(line == 1, pull, 0.0)).T
    return columns[:, 0:1], columns[:, 1:2]


def ahead_kernel(
    members, stats_ref, attention_ref, gated_ref, scaled_ref, q_ref, early_ref, grad_ref, out_ref
):
    rows, features = attention_ref.shape
    heads = features // DH
    step = out_ref.shape[0] // members
    chunk = step - 1
    inverse, pull = token_scales(stats_ref)
    for head in range(heads):
        at = cols(head)
        attention = attention_ref[:, at]
        grad = (inverse * scaled_ref[:, at] - pull * attention).astype(half)
        grad_ref[:, at] = grad
        ahead = dot(twice(q_ref[:, at].T, 1), halves(early_ref[:, at] * grad.astype(wide), 0))
        for piece in range(DH // chunk):
            start = (head * (DH // chunk) + piece) * step
            out_ref[start : start + chunk, :] = ahead[piece * chunk : (piece + 1) * chunk, :]
        gain_row = jnp.sum(gated_ref[:, at] * (attention * inverse), axis=0, keepdims=True)
        for block in range(head, members, heads):
            out_ref[block * step + chunk : (block + 1) * step, :] = gain_row


def early_grads_kernel(
    spans_ref, stats_ref, attention_ref, scaled_ref, gate_ref, grad_ref, q_ref, k_ref, v_ref,
    weights_ref, prefix_ref, early_ref, grad_q_ref, grad_gate_ref, local_k_ref, local_v_ref, late_ref,
):
    rows, features = q_ref.shape
    inverse, _ = token_scales(stats_ref)
    for head in range(features // DH):
        at = cols(head)
        normed = attention_ref[:, at] * inverse
        rest = 1.0 - jax.nn.sigmoid(gate_ref[:, at].astype(wide))
        grad_gate_ref[:, at] = (scaled_ref[:, at] * normed * rest).astype(half)
        grad = grad_ref[:, at]
        rate = spans_ref[8 + head : 9 + head, :]
        late_ref[:, at] = decay_column(rate, rows, True) * (1.0 / DH)
        square = decay_square(rate, rows)
        grad_scores = (dot_nt(grad, v_ref[:, at]) * square).astype(half)
        carried = dot_nt(twice(grad, 1), halves(prefix_ref[at, :], 1)) * (1.0 / DH)
        grad_q = dot(grad_scores, k_ref[:, at]) + early_ref[:, at] * carried
        grad_q_ref[:, at] = grad_q.astype(half)
        local_k_ref[:, at] = dot_tn(grad_scores, q_ref[:, at])
        local_v_ref[:, at] = dot_tn(weights_ref[:, at], grad)


def final_kernel(
    members, back_ref, k_ref, v_ref, local_k_ref, local_v_ref, late_ref, grad_k_ref, grad_v_ref, gain_ref,
    keys, values, gain, left,
):
    rows, features = k_ref.shape
    heads = features // DH
    copies = []

    def send(source, target):
        copy = pltpu.make_async_copy(source, target, left.at[len(copies)])
        copy.start()
        copies.append(copy)

    step = back_ref.shape[0] // members
    chunk = step - 1
    pieces = DH // chunk
    for head in range(heads):
        gain[:, cols(head)] = back_ref[head * step + chunk : (head + 1) * step, :]
    send(gain, gain_ref)
    for head in range(heads):
        at = cols(head)
        late = late_ref[:, at]
        starts = [block * step for block in range(head * pieces, (head + 1) * pieces)]
        suffix = jnp.concatenate([back_ref[start : start + chunk, :] for start in starts], axis=0)
        high = suffix.astype(half)
        low = (suffix - high.astype(wide)).astype(half)
        carried_k = dot_nt(twice(v_ref[:, at], 1), jnp.concatenate([high, low], axis=1))
        carried_v = dot(twice(k_ref[:, at], 1), jnp.concatenate([high, low], axis=0))
        keys[:, at] = (local_k_ref[:, at] + late * carried_k).astype(half)
        send(keys.at[:, at], grad_k_ref.at[:, at])
        values[:, at] = (local_v_ref[:, at] + late * carried_v).astype(half)
        send(values.at[:, at], grad_v_ref.at[:, at])
    for copy in copies:
        copy.wait()


def call(kernel, name, shapes, *operands, place=pltpu.VMEM, out_place=pltpu.VMEM, scratch=(), flops=0, bytes_moved=0):
    out_shape = [jax.ShapeDtypeStruct(*shape) for shape in shapes]
    results = pl.pallas_call(
        kernel,
        out_shape=out_shape,
        in_specs=[pl.BlockSpec(memory_space=place)] * len(operands),
        out_specs=[pl.BlockSpec(memory_space=out_place)] * len(out_shape),
        scratch_shapes=list(scratch),
        compiler_params=pltpu.CompilerParams(vmem_limit_bytes=24 * 1024 * 1024),
        cost_estimate=pl.CostEstimate(flops=flops, bytes_accessed=bytes_moved, transcendentals=0),
        name=name,
    )(*operands)
    return results if len(out_shape) > 1 else results[0]


def body(queries, key_rows, value_rows, gate_in, grad_out, decay_ints, norm_gain):
    rows, features = queries.shape
    members = lax.axis_size("ctx")
    head_members = lax.axis_size("head")
    chunk = features // members
    step = chunk + 1
    area = rows * features
    flat = ((features, DH), wide)
    long = ((members * step, DH), wide)
    block_wide = ((rows, features), wide)
    block_half = ((rows, features), half)

    def across(array, width):
        shape = (members, width, DH) if width % 8 == 0 else (members, width, 1, DH)
        return swap(array.reshape(shape), "ctx").reshape(members * width, DH)

    def sized(kernel):
        return functools.partial(kernel, members)

    given = (decay_ints, key_rows, value_rows, norm_gain.reshape(1, features))
    summary, spans, gain = call(
        sized(summary_kernel),
        "summary",
        [flat, ((16, DH), wide), ((1, features), wide)],
        *[pltpu.with_memory_space_constraint(a, pltpu.HBM) for a in given],
        place=pltpu.HBM,
        scratch=[
            pltpu.SMEM(decay_ints.shape, jnp.int32),
            pltpu.VMEM((rows, features), half),
            pltpu.VMEM((rows, features), half),
            pltpu.VMEM((rows, features), wide),
            pltpu.SemaphoreType.DMA((4,)),
        ],
    )
    there = across(summary, chunk)
    prefix = across(call(sized(forward_kernel), "forward_scan", [flat], spans, there), chunk)
    attention, stats, weights, gated, scaled, early = call(
        attend_kernel,
        "attend",
        [block_wide, ((head_members, 8, rows), wide), block_half, block_wide, block_wide, block_wide],
        spans, queries, key_rows, value_rows, gate_in, grad_out, gain, prefix,
    )
    stats = swap(stats, "head")
    grad, message = call(
        sized(ahead_kernel),
        "ahead",
        [block_half, long],
        stats, attention, gated, scaled, queries, early,
    )
    there = across(message, step)
    grad_q, grad_gate, local_k, local_v, late = call(
        early_grads_kernel,
        "early_grads",
        [block_half, block_half, block_wide, block_wide, block_wide],
        spans, stats, attention, scaled, gate_in, grad, queries, key_rows, value_rows,
        weights, prefix, early,
        flops=20 * area * DH, bytes_moved=28 * area,
    )
    back = across(call(sized(backward_kernel), "backward_scan", [long], spans, there), step)
    grad_k, grad_v, grad_gain = call(
        sized(final_kernel),
        "final",
        [block_half, block_half, ((1, features), wide)],
        back, key_rows, value_rows, local_k, local_v, late,
        out_place=pltpu.HBM,
        scratch=[
            pltpu.VMEM((rows, features), half),
            pltpu.VMEM((rows, features), half),
            pltpu.VMEM((1, features), wide),
            pltpu.SemaphoreType.DMA((2 * features // DH + 1,)),
        ],
    )
    return grad_q, grad_k, grad_v, grad_gate, grad_gain.reshape(features)


def solution(mesh):
    placed = (
        P("ctx", "head"),
        P("ctx", "head"),
        P("ctx", "head"),
        P("ctx", "head"),
        P("ctx", "head"),
        P("head"),
        P("head"),
    )
    return jax.shard_map(
        body,
        mesh=mesh,
        in_specs=placed,
        out_specs=(
            P("ctx", "head"),
            P("ctx", "head"),
            P("ctx", "head"),
            P("ctx", "head"),
            P("head"),
        ),
        check_vma=False,
    )
```

```python
import functools

import jax
import jax.numpy as jnp
from jax import lax
from jax.experimental import pallas as pl
from jax.experimental.pallas import tpu as pltpu
from jax.sharding import PartitionSpec as P

DH = 128
HD = 8192


rate_unit = 2.0 ** (-20)
norm_eps = 1e-06
first_place = {"ctx": 36, "head": 14}
wide = jnp.float32
half = jnp.bfloat16


def swap(array, axis):
    size, first = lax.axis_size(axis), first_place[axis]
    groups = [[(first + slot) % size for slot in range(size)]]
    return lax.all_to_all(array, axis, 0, 0, axis_index_groups=groups)


def ctx_slots(members):
    return [(block - first_place["ctx"]) % members for block in range(members)]


def halves(array, axis):
    high = array.astype(half)
    low = (array - high.astype(wide)).astype(half)
    return jnp.concatenate([high, low], axis=axis)


def twice(array, axis):
    return jnp.concatenate([array, array], axis=axis)


def dot(left, right):
    return jnp.dot(left, right, preferred_element_type=wide)


def dot_nt(left, right):
    return lax.dot_general(left, right, (((1,), (1,)), ((), ())), preferred_element_type=wide)


def dot_tn(left, right):
    return lax.dot_general(left, right, (((0,), (0,)), ((), ())), preferred_element_type=wide)


def rate_of(ints_ref, head):
    return ints_ref[head].astype(wide) * rate_unit


def decay_column(rate, rows, late):
    place = lax.broadcasted_iota(jnp.int32, (rows, DH), 0).astype(wide)
    return jnp.exp(-rate * ((rows - 1.0 - place) if late else (place + 1.0)))


def decay_square(rate, rows):
    later = lax.broadcasted_iota(jnp.int32, (rows, rows), 0)
    sooner = lax.broadcasted_iota(jnp.int32, (rows, rows), 1)
    gap = (later - sooner).astype(wide)
    return jnp.where(gap >= 0.0, jnp.exp(-rate * jnp.maximum(gap, 0.0)), 0.0) * (1.0 / DH)


def cols(head):
    return slice(head * DH, (head + 1) * DH)


def summary_kernel(
    members, ints_ref, k_ref, v_ref, gain_ref, out_ref, spans_ref, gain_out_ref, ints, keys, values, late, arrived
):
    rows, features = k_ref.shape
    heads = features // DH
    copies = [
        pltpu.make_async_copy(source, target, arrived.at[number])
        for number, (source, target) in enumerate(
            ((ints_ref, ints), (k_ref, keys), (v_ref, values), (gain_ref, gain_out_ref))
        )
    ]
    for copy in copies:
        copy.start()
    copies[0].wait()
    slot = (lax.axis_index("ctx") + (members - first_place["ctx"])) % members
    owned = slot * (features // members) // DH
    power = lax.broadcasted_iota(jnp.int32, (8, DH), 0).astype(wide) + 1.0
    spans_ref[0:8, :] = jnp.exp(-(rate_of(ints, owned) * rows) * power)
    for head in range(heads):
        spans_ref[8 + head : 9 + head, :] = jnp.full((1, DH), rate_of(ints, head), wide)
        late[:, cols(head)] = decay_column(rate_of(ints, head), rows, True)
    copies[1].wait()
    copies[2].wait()
    for head in range(heads):
        weighted = late[:, cols(head)] * values[:, cols(head)].astype(wide)
        out_ref[cols(head), :] = dot(twice(keys[:, cols(head)].T, 1), halves(weighted, 0))
    copies[3].wait()


def scan_blocks(order, span, leap, take, put, zero):
    chains = [order[at : at + 8] for at in range(0, len(order), 8)]
    totals = [take(chain[0]) for chain in chains]
    for turn in range(1, 8):
        blocks = [take(chain[turn]) for chain in chains]
        totals = [span * total + block for total, block in zip(totals, blocks)]
    states = [zero]
    for total in totals[:-1]:
        states.append(leap * states[-1] + total)
    for turn in range(8):
        blocks = [take(chain[turn]) for chain in chains]
        for chain, state in zip(chains, states):
            put(chain[turn], state)
        states = [span * state + block for state, block in zip(states, blocks)]


def forward_kernel(members, spans_ref, in_ref, out_ref):
    chunk = in_ref.shape[0] // members

    def take(block):
        return in_ref[block * chunk : (block + 1) * chunk, :]

    def put(block, state):
        out_ref[block * chunk : (block + 1) * chunk, :] = state

    order = ctx_slots(members)
    scan_blocks(order, spans_ref[0:1, :], spans_ref[7:8, :], take, put, jnp.zeros((chunk, DH), wide))


def backward_kernel(members, spans_ref, in_ref, out_ref):
    step = in_ref.shape[0] // members
    chunk = step - 1

    def take(block):
        return in_ref[block * step : block * step + chunk, :]

    def put(block, state):
        out_ref[block * step : block * step + chunk, :] = state

    order = list(reversed(ctx_slots(members)))
    scan_blocks(order, spans_ref[0:1, :], spans_ref[7:8, :], take, put, jnp.zeros((chunk, DH), wide))
    gains = [in_ref[block * step + chunk : (block + 1) * step, :] for block in range(members)]
    while len(gains) > 1:
        gains = [gains[at] + gains[at + 1] for at in range(0, len(gains), 2)]
    for block in range(members):
        out_ref[block * step + chunk : (block + 1) * step, :] = gains[0]


def attend_kernel(
    spans_ref, q_ref, k_ref, v_ref, gate_ref, grad_ref, gain_ref, prefix_ref,
    attention_ref, stats_ref, weights_ref, gated_ref, scaled_ref, early_ref,
):
    rows, features = q_ref.shape
    squares = jnp.zeros((rows, DH), wide)
    crossed = jnp.zeros((rows, DH), wide)
    for head in range(features // DH):
        at = cols(head)
        rate = spans_ref[8 + head : 9 + head, :]
        queries = q_ref[:, at]
        weights = (dot_nt(queries, k_ref[:, at]) * decay_square(rate, rows)).astype(half)
        weights_ref[:, at] = weights
        gated = grad_ref[:, at].astype(wide) * jax.nn.sigmoid(gate_ref[:, at].astype(wide))
        gated_ref[:, at] = gated
        scaled = gated * gain_ref[:, at]
        scaled_ref[:, at] = scaled
        early = decay_column(rate, rows, False)
        early_ref[:, at] = early
        carried = dot(twice(queries, 1), halves(prefix_ref[at, :], 0)) * (1.0 / DH)
        attention = dot(weights, v_ref[:, at]) + early * carried
        attention_ref[:, at] = attention
        squares = squares + attention * attention
        crossed = crossed + scaled * attention
    squares = jnp.sum(squares.T, axis=0, keepdims=True)
    crossed = jnp.sum(crossed.T, axis=0, keepdims=True)
    line = lax.broadcasted_iota(jnp.int32, (8, DH), 0)
    pair = jnp.where(line == 0, squares, jnp.where(line == 1, crossed, 0.0))
    for member in range(stats_ref.shape[0]):
        stats_ref[member] = pair


def token_scales(stats_ref):
    total = stats_ref[0]
    for member in range(1, stats_ref.shape[0]):
        total = total + stats_ref[member]
    inverse = lax.rsqrt(total[0:1] * (1.0 / HD) + norm_eps)
    pull = inverse * inverse * inverse * total[1:2] * (1.0 / HD)
    line = lax.broadcasted_iota(jnp.int32, (8, DH), 0)
    columns = jnp.where(line == 0, inverse, jnp.where(line == 1, pull, 0.0)).T
    return columns[:, 0:1], columns[:, 1:2]


def ahead_kernel(
    members, stats_ref, attention_ref, gated_ref, scaled_ref, q_ref, early_ref, grad_ref, out_ref
):
    rows, features = attention_ref.shape
    heads = features // DH
    step = out_ref.shape[0] // members
    chunk = step - 1
    inverse, pull = token_scales(stats_ref)
    for head in range(heads):
        at = cols(head)
        attention = attention_ref[:, at]
        grad = (inverse * scaled_ref[:, at] - pull * attention).astype(half)
        grad_ref[:, at] = grad
        ahead = dot(twice(q_ref[:, at].T, 1), halves(early_ref[:, at] * grad.astype(wide), 0))
        for piece in range(DH // chunk):
            start = (head * (DH // chunk) + piece) * step
            out_ref[start : start + chunk, :] = ahead[piece * chunk : (piece + 1) * chunk, :]
        gain_row = jnp.sum(gated_ref[:, at] * (attention * inverse), axis=0, keepdims=True)
        for block in range(head, members, heads):
            out_ref[block * step + chunk : (block + 1) * step, :] = gain_row


def early_grads_kernel(
    spans_ref, stats_ref, attention_ref, scaled_ref, gate_ref, grad_ref, q_ref, k_ref, v_ref,
    weights_ref, prefix_ref, early_ref, grad_q_ref, grad_gate_ref, local_k_ref, local_v_ref, late_ref, spans_out_ref,
):
    rows, features = q_ref.shape
    spans_out_ref[...] = spans_ref[...]
    inverse, _ = token_scales(stats_ref)
    for head in range(features // DH):
        at = cols(head)
        normed = attention_ref[:, at] * inverse
        rest = 1.0 - jax.nn.sigmoid(gate_ref[:, at].astype(wide))
        grad_gate_ref[:, at] = (scaled_ref[:, at] * normed * rest).astype(half)
        grad = grad_ref[:, at]
        rate = spans_ref[8 + head : 9 + head, :]
        late_ref[:, at] = decay_column(rate, rows, True) * (1.0 / DH)
        square = decay_square(rate, rows)
        grad_scores = (dot_nt(grad, v_ref[:, at]) * square).astype(half)
        carried = dot_nt(twice(grad, 1), halves(prefix_ref[at, :], 1)) * (1.0 / DH)
        grad_q = dot(grad_scores, k_ref[:, at]) + early_ref[:, at] * carried
        grad_q_ref[:, at] = grad_q.astype(half)
        local_k_ref[:, at] = dot_tn(grad_scores, q_ref[:, at])
        local_v_ref[:, at] = dot_tn(weights_ref[:, at], grad)


def final_kernel(
    members, back_ref, k_ref, v_ref, local_k_ref, local_v_ref, late_ref, grad_k_ref, grad_v_ref, gain_ref,
    keys, values, gain, left,
):
    rows, features = k_ref.shape
    heads = features // DH
    copies = []

    def send(source, target):
        copy = pltpu.make_async_copy(source, target, left.at[len(copies)])
        copy.start()
        copies.append(copy)

    step = back_ref.shape[0] // members
    chunk = step - 1
    pieces = DH // chunk
    for head in range(heads):
        gain[:, cols(head)] = back_ref[head * step + chunk : (head + 1) * step, :]
    send(gain, gain_ref)
    for head in range(heads):
        at = cols(head)
        late = late_ref[:, at]
        starts = [block * step for block in range(head * pieces, (head + 1) * pieces)]
        suffix = jnp.concatenate([back_ref[start : start + chunk, :] for start in starts], axis=0)
        high = suffix.astype(half)
        low = (suffix - high.astype(wide)).astype(half)
        carried_k = dot_nt(twice(v_ref[:, at], 1), jnp.concatenate([high, low], axis=1))
        carried_v = dot(twice(k_ref[:, at], 1), jnp.concatenate([high, low], axis=0))
        keys[:, at] = (local_k_ref[:, at] + late * carried_k).astype(half)
        send(keys.at[:, at], grad_k_ref.at[:, at])
        values[:, at] = (local_v_ref[:, at] + late * carried_v).astype(half)
        send(values.at[:, at], grad_v_ref.at[:, at])
    for copy in copies:
        copy.wait()


def call(kernel, name, shapes, *operands, place=pltpu.VMEM, out_place=pltpu.VMEM, scratch=(), flops=0, bytes_moved=0):
    out_shape = [jax.ShapeDtypeStruct(*shape) for shape in shapes]
    results = pl.pallas_call(
        kernel,
        out_shape=out_shape,
        in_specs=[pl.BlockSpec(memory_space=place)] * len(operands),
        out_specs=[pl.BlockSpec(memory_space=out_place)] * len(out_shape),
        scratch_shapes=list(scratch),
        compiler_params=pltpu.CompilerParams(vmem_limit_bytes=24 * 1024 * 1024),
        cost_estimate=pl.CostEstimate(flops=flops, bytes_accessed=bytes_moved, transcendentals=0),
        name=name,
    )(*operands)
    return results if len(out_shape) > 1 else results[0]


def body(queries, key_rows, value_rows, gate_in, grad_out, decay_ints, norm_gain):
    rows, features = queries.shape
    members = lax.axis_size("ctx")
    head_members = lax.axis_size("head")
    chunk = features // members
    step = chunk + 1
    area = rows * features
    flat = ((features, DH), wide)
    long = ((members * step, DH), wide)
    block_wide = ((rows, features), wide)
    block_half = ((rows, features), half)

    def across(array, width):
        shape = (members, width, DH) if width % 8 == 0 else (members, width, 1, DH)
        return swap(array.reshape(shape), "ctx").reshape(members * width, DH)

    def sized(kernel):
        return functools.partial(kernel, members)

    given = (decay_ints, key_rows, value_rows, norm_gain.reshape(1, features))
    summary, spans, gain = call(
        sized(summary_kernel),
        "summary",
        [flat, ((16, DH), wide), ((1, features), wide)],
        *[pltpu.with_memory_space_constraint(a, pltpu.HBM) for a in given],
        place=pltpu.HBM,
        scratch=[
            pltpu.SMEM(decay_ints.shape, jnp.int32),
            pltpu.VMEM((rows, features), half),
            pltpu.VMEM((rows, features), half),
            pltpu.VMEM((rows, features), wide),
            pltpu.SemaphoreType.DMA((4,)),
        ],
    )
    there = across(summary, chunk)
    prefix = across(call(sized(forward_kernel), "forward_scan", [flat], spans, there), chunk)
    attention, stats, weights, gated, scaled, early = call(
        attend_kernel,
        "attend",
        [block_wide, ((head_members, 8, rows), wide), block_half, block_wide, block_wide, block_wide],
        spans, queries, key_rows, value_rows, gate_in, grad_out, gain, prefix,
    )
    stats = swap(stats, "head")
    grad, message = call(
        sized(ahead_kernel),
        "ahead",
        [block_half, long],
        stats, attention, gated, scaled, queries, early,
    )
    there = across(message, step)
    grad_q, grad_gate, local_k, local_v, late, spans = call(
        early_grads_kernel,
        "early_grads",
        [block_half, block_half, block_wide, block_wide, block_wide, (spans.shape, wide)],
        spans, stats, attention, scaled, gate_in, grad, queries, key_rows, value_rows,
        weights, prefix, early,
        flops=20 * area * DH, bytes_moved=28 * area,
    )
    back = across(call(sized(backward_kernel), "backward_scan", [long], spans, there), step)
    grad_k, grad_v, grad_gain = call(
        sized(final_kernel),
        "final",
        [block_half, block_half, ((1, features), wide)],
        back, key_rows, value_rows, local_k, local_v, late,
        out_place=pltpu.HBM,
        scratch=[
            pltpu.VMEM((rows, features), half),
            pltpu.VMEM((rows, features), half),
            pltpu.VMEM((1, features), wide),
            pltpu.SemaphoreType.DMA((2 * features // DH + 1,)),
        ],
    )
    return grad_q, grad_k, grad_v, grad_gate, grad_gain.reshape(features)


def solution(mesh):
    placed = (
        P("ctx", "head"),
        P("ctx", "head"),
        P("ctx", "head"),
        P("ctx", "head"),
        P("ctx", "head"),
        P("head"),
        P("head"),
    )
    return jax.shard_map(
        body,
        mesh=mesh,
        in_specs=placed,
        out_specs=(
            P("ctx", "head"),
            P("ctx", "head"),
            P("ctx", "head"),
            P("ctx", "head"),
            P("head"),
        ),
        check_vma=False,
    )
```

```python
import functools

import jax
import jax.numpy as jnp
from jax import lax
from jax.experimental import pallas as pl
from jax.experimental.pallas import tpu as pltpu
from jax.sharding import PartitionSpec as P

DH = 128
HD = 8192


rate_unit = 2.0 ** (-20)
norm_eps = 1e-06
first_place = {"ctx": 36, "head": 14}
wide = jnp.float32
half = jnp.bfloat16


def swap(array, axis):
    size, first = lax.axis_size(axis), first_place[axis]
    groups = [[(first + slot) % size for slot in range(size)]]
    return lax.all_to_all(array, axis, 0, 0, axis_index_groups=groups)


def ctx_slots(members):
    return [(block - first_place["ctx"]) % members for block in range(members)]


def halves(array, axis):
    high = array.astype(half)
    low = (array - high.astype(wide)).astype(half)
    return jnp.concatenate([high, low], axis=axis)


def twice(array, axis):
    return jnp.concatenate([array, array], axis=axis)


def dot(left, right):
    return jnp.dot(left, right, preferred_element_type=wide)


def dot_nt(left, right):
    return lax.dot_general(left, right, (((1,), (1,)), ((), ())), preferred_element_type=wide)


def dot_tn(left, right):
    return lax.dot_general(left, right, (((0,), (0,)), ((), ())), preferred_element_type=wide)


def rate_of(ints_ref, head):
    return ints_ref[head].astype(wide) * rate_unit


def decay_column(rate, rows, late):
    place = lax.broadcasted_iota(jnp.int32, (rows, DH), 0).astype(wide)
    return jnp.exp(-rate * ((rows - 1.0 - place) if late else (place + 1.0)))


def decay_square(rate, rows):
    later = lax.broadcasted_iota(jnp.int32, (rows, rows), 0)
    sooner = lax.broadcasted_iota(jnp.int32, (rows, rows), 1)
    gap = (later - sooner).astype(wide)
    return jnp.where(gap >= 0.0, jnp.exp(-rate * jnp.maximum(gap, 0.0)), 0.0) * (1.0 / DH)


def cols(head):
    return slice(head * DH, (head + 1) * DH)


def summary_kernel(
    members, ints_ref, k_ref, v_ref, gain_ref, out_ref, spans_ref, gain_out_ref, ints, keys, values, late, arrived
):
    rows, features = k_ref.shape
    heads = features // DH
    copies = [
        pltpu.make_async_copy(source, target, arrived.at[number])
        for number, (source, target) in enumerate(
            ((ints_ref, ints), (k_ref, keys), (v_ref, values), (gain_ref, gain_out_ref))
        )
    ]
    for copy in copies:
        copy.start()
    copies[0].wait()
    slot = (lax.axis_index("ctx") + (members - first_place["ctx"])) % members
    owned = slot * (features // members) // DH
    power = lax.broadcasted_iota(jnp.int32, (8, DH), 0).astype(wide) + 1.0
    spans_ref[0:8, :] = jnp.exp(-(rate_of(ints, owned) * rows) * power)
    for head in range(heads):
        spans_ref[8 + head : 9 + head, :] = jnp.full((1, DH), rate_of(ints, head), wide)
        late[:, cols(head)] = decay_column(rate_of(ints, head), rows, True)
    copies[1].wait()
    copies[2].wait()
    for head in range(heads):
        weighted = late[:, cols(head)] * values[:, cols(head)].astype(wide)
        out_ref[cols(head), :] = dot(twice(keys[:, cols(head)].T, 1), halves(weighted, 0))
    copies[3].wait()


def scan_blocks(order, span, leap, take, put, zero):
    chains = [order[at : at + 8] for at in range(0, len(order), 8)]
    totals = [take(chain[0]) for chain in chains]
    for turn in range(1, 8):
        blocks = [take(chain[turn]) for chain in chains]
        totals = [span * total + block for total, block in zip(totals, blocks)]
    states = [zero]
    for total in totals[:-1]:
        states.append(leap * states[-1] + total)
    for turn in range(8):
        blocks = [take(chain[turn]) for chain in chains]
        for chain, state in zip(chains, states):
            put(chain[turn], state)
        states = [span * state + block for state, block in zip(states, blocks)]


def forward_kernel(members, spans_ref, in_ref, out_ref):
    chunk = in_ref.shape[0] // members

    def take(block):
        return in_ref[block * chunk : (block + 1) * chunk, :]

    def put(block, state):
        out_ref[block * chunk : (block + 1) * chunk, :] = state

    order = ctx_slots(members)
    scan_blocks(order, spans_ref[0:1, :], spans_ref[7:8, :], take, put, jnp.zeros((chunk, DH), wide))


def backward_kernel(members, spans_ref, in_ref, out_ref):
    step = in_ref.shape[0] // members
    chunk = step - 1

    def take(block):
        return in_ref[block * step : block * step + chunk, :]

    def put(block, state):
        out_ref[block * step : block * step + chunk, :] = state

    order = list(reversed(ctx_slots(members)))
    scan_blocks(order, spans_ref[0:1, :], spans_ref[7:8, :], take, put, jnp.zeros((chunk, DH), wide))
    gains = [in_ref[block * step + chunk : (block + 1) * step, :] for block in range(members)]
    while len(gains) > 1:
        gains = [gains[at] + gains[at + 1] for at in range(0, len(gains), 2)]
    for block in range(members):
        out_ref[block * step + chunk : (block + 1) * step, :] = gains[0]


def attend_kernel(
    spans_ref, q_ref, k_ref, v_ref, gate_ref, grad_ref, gain_ref, prefix_ref,
    attention_ref, stats_ref, weights_ref, gated_ref, scaled_ref, early_ref,
):
    rows, features = q_ref.shape
    squares = jnp.zeros((rows, DH), wide)
    crossed = jnp.zeros((rows, DH), wide)
    for head in range(features // DH):
        at = cols(head)
        rate = spans_ref[8 + head : 9 + head, :]
        queries = q_ref[:, at]
        weights = (dot_nt(queries, k_ref[:, at]) * decay_square(rate, rows)).astype(half)
        weights_ref[:, at] = weights
        gated = grad_ref[:, at].astype(wide) * jax.nn.sigmoid(gate_ref[:, at].astype(wide))
        gated_ref[:, at] = gated
        scaled = gated * gain_ref[:, at]
        scaled_ref[:, at] = scaled
        early = decay_column(rate, rows, False)
        early_ref[:, at] = early
        carried = dot(twice(queries, 1), halves(prefix_ref[at, :], 0)) * (1.0 / DH)
        attention = dot(weights, v_ref[:, at]) + early * carried
        attention_ref[:, at] = attention
        squares = squares + attention * attention
        crossed = crossed + scaled * attention
    squares = jnp.sum(squares.T, axis=0, keepdims=True)
    crossed = jnp.sum(crossed.T, axis=0, keepdims=True)
    pair = jnp.concatenate([squares, crossed], axis=0)
    for member in range(stats_ref.shape[0]):
        stats_ref[member] = pair


def token_scales(stats_ref):
    total = jnp.sum(stats_ref[...], axis=0)
    inverse = lax.rsqrt(total[0:1] * (1.0 / HD) + norm_eps)
    pull = inverse * inverse * inverse * total[1:2] * (1.0 / HD)
    line = lax.broadcasted_iota(jnp.int32, (8, DH), 0)
    columns = jnp.where(line == 0, inverse, jnp.where(line == 1, pull, 0.0)).T
    return columns[:, 0:1], columns[:, 1:2]


def ahead_kernel(
    members, stats_ref, attention_ref, gated_ref, scaled_ref, q_ref, early_ref, grad_ref, out_ref
):
    rows, features = attention_ref.shape
    heads = features // DH
    step = out_ref.shape[0] // members
    chunk = step - 1
    inverse, pull = token_scales(stats_ref)
    for head in range(heads):
        at = cols(head)
        attention = attention_ref[:, at]
        grad = (inverse * scaled_ref[:, at] - pull * attention).astype(half)
        grad_ref[:, at] = grad
        ahead = dot(twice(q_ref[:, at].T, 1), halves(early_ref[:, at] * grad.astype(wide), 0))
        for piece in range(DH // chunk):
            start = (head * (DH // chunk) + piece) * step
            out_ref[start : start + chunk, :] = ahead[piece * chunk : (piece + 1) * chunk, :]
        gain_row = jnp.sum(gated_ref[:, at] * (attention * inverse), axis=0, keepdims=True)
        for block in range(head, members, heads):
            out_ref[block * step + chunk : (block + 1) * step, :] = gain_row


def early_grads_kernel(
    spans_ref, stats_ref, attention_ref, scaled_ref, gate_ref, grad_ref, q_ref, k_ref, v_ref,
    weights_ref, prefix_ref, early_ref, grad_q_ref, grad_gate_ref, local_k_ref, local_v_ref, late_ref,
):
    rows, features = q_ref.shape
    inverse, _ = token_scales(stats_ref)
    for head in range(features // DH):
        at = cols(head)
        normed = attention_ref[:, at] * inverse
        rest = 1.0 - jax.nn.sigmoid(gate_ref[:, at].astype(wide))
        grad_gate_ref[:, at] = (scaled_ref[:, at] * normed * rest).astype(half)
        grad = grad_ref[:, at]
        rate = spans_ref[8 + head : 9 + head, :]
        late_ref[:, at] = decay_column(rate, rows, True) * (1.0 / DH)
        square = decay_square(rate, rows)
        grad_scores = (dot_nt(grad, v_ref[:, at]) * square).astype(half)
        carried = dot_nt(twice(grad, 1), halves(prefix_ref[at, :], 1)) * (1.0 / DH)
        grad_q = dot(grad_scores, k_ref[:, at]) + early_ref[:, at] * carried
        grad_q_ref[:, at] = grad_q.astype(half)
        local_k_ref[:, at] = dot_tn(grad_scores, q_ref[:, at])
        local_v_ref[:, at] = dot_tn(weights_ref[:, at], grad)


def final_kernel(
    members, back_ref, k_ref, v_ref, local_k_ref, local_v_ref, late_ref, grad_k_ref, grad_v_ref, gain_ref,
    keys, values, gain, left,
):
    rows, features = k_ref.shape
    heads = features // DH
    copies = []

    def send(source, target):
        copy = pltpu.make_async_copy(source, target, left.at[len(copies)])
        copy.start()
        copies.append(copy)

    step = back_ref.shape[0] // members
    chunk = step - 1
    pieces = DH // chunk
    for head in range(heads):
        gain[:, cols(head)] = back_ref[head * step + chunk : (head + 1) * step, :]
    send(gain, gain_ref)
    for head in range(heads):
        at = cols(head)
        late = late_ref[:, at]
        starts = [block * step for block in range(head * pieces, (head + 1) * pieces)]
        suffix = jnp.concatenate([back_ref[start : start + chunk, :] for start in starts], axis=0)
        high = suffix.astype(half)
        low = (suffix - high.astype(wide)).astype(half)
        carried_k = dot_nt(twice(v_ref[:, at], 1), jnp.concatenate([high, low], axis=1))
        carried_v = dot(twice(k_ref[:, at], 1), jnp.concatenate([high, low], axis=0))
        keys[:, at] = (local_k_ref[:, at] + late * carried_k).astype(half)
        send(keys.at[:, at], grad_k_ref.at[:, at])
        values[:, at] = (local_v_ref[:, at] + late * carried_v).astype(half)
        send(values.at[:, at], grad_v_ref.at[:, at])
    for copy in copies:
        copy.wait()


def call(kernel, name, shapes, *operands, place=pltpu.VMEM, out_place=pltpu.VMEM, scratch=(), flops=0, bytes_moved=0):
    out_shape = [jax.ShapeDtypeStruct(*shape) for shape in shapes]
    results = pl.pallas_call(
        kernel,
        out_shape=out_shape,
        in_specs=[pl.BlockSpec(memory_space=place)] * len(operands),
        out_specs=[pl.BlockSpec(memory_space=out_place)] * len(out_shape),
        scratch_shapes=list(scratch),
        compiler_params=pltpu.CompilerParams(vmem_limit_bytes=24 * 1024 * 1024),
        cost_estimate=pl.CostEstimate(flops=flops, bytes_accessed=bytes_moved, transcendentals=0),
        name=name,
    )(*operands)
    return results if len(out_shape) > 1 else results[0]


def body(queries, key_rows, value_rows, gate_in, grad_out, decay_ints, norm_gain):
    rows, features = queries.shape
    members = lax.axis_size("ctx")
    head_members = lax.axis_size("head")
    chunk = features // members
    step = chunk + 1
    area = rows * features
    flat = ((features, DH), wide)
    long = ((members * step, DH), wide)
    block_wide = ((rows, features), wide)
    block_half = ((rows, features), half)

    def across(array, width):
        shape = (members, width, DH) if width % 8 == 0 else (members, width, 1, DH)
        return swap(array.reshape(shape), "ctx").reshape(members * width, DH)

    def sized(kernel):
        return functools.partial(kernel, members)

    given = (decay_ints, key_rows, value_rows, norm_gain.reshape(1, features))
    summary, spans, gain = call(
        sized(summary_kernel),
        "summary",
        [flat, ((16, DH), wide), ((1, features), wide)],
        *[pltpu.with_memory_space_constraint(a, pltpu.HBM) for a in given],
        place=pltpu.HBM,
        scratch=[
            pltpu.SMEM(decay_ints.shape, jnp.int32),
            pltpu.VMEM((rows, features), half),
            pltpu.VMEM((rows, features), half),
            pltpu.VMEM((rows, features), wide),
            pltpu.SemaphoreType.DMA((4,)),
        ],
    )
    there = across(summary, chunk)
    prefix = across(call(sized(forward_kernel), "forward_scan", [flat], spans, there), chunk)
    attention, stats, weights, gated, scaled, early = call(
        attend_kernel,
        "attend",
        [block_wide, ((head_members, 2, rows), wide), block_half, block_wide, block_wide, block_wide],
        spans, queries, key_rows, value_rows, gate_in, grad_out, gain, prefix,
    )
    stats = swap(stats, "head")
    grad, message = call(
        sized(ahead_kernel),
        "ahead",
        [block_half, long],
        stats, attention, gated, scaled, queries, early,
    )
    there = across(message, step)
    grad_q, grad_gate, local_k, local_v, late = call(
        early_grads_kernel,
        "early_grads",
        [block_half, block_half, block_wide, block_wide, block_wide],
        spans, stats, attention, scaled, gate_in, grad, queries, key_rows, value_rows,
        weights, prefix, early,
        flops=20 * area * DH, bytes_moved=28 * area,
    )
    back = across(call(sized(backward_kernel), "backward_scan", [long], spans, there), step)
    grad_k, grad_v, grad_gain = call(
        sized(final_kernel),
        "final",
        [block_half, block_half, ((1, features), wide)],
        back, key_rows, value_rows, local_k, local_v, late,
        out_place=pltpu.HBM,
        scratch=[
            pltpu.VMEM((rows, features), half),
            pltpu.VMEM((rows, features), half),
            pltpu.VMEM((1, features), wide),
            pltpu.SemaphoreType.DMA((2 * features // DH + 1,)),
        ],
    )
    return grad_q, grad_k, grad_v, grad_gate, grad_gain.reshape(features)


def solution(mesh):
    placed = (
        P("ctx", "head"),
        P("ctx", "head"),
        P("ctx", "head"),
        P("ctx", "head"),
        P("ctx", "head"),
        P("head"),
        P("head"),
    )
    return jax.shard_map(
        body,
        mesh=mesh,
        in_specs=placed,
        out_specs=(
            P("ctx", "head"),
            P("ctx", "head"),
            P("ctx", "head"),
            P("ctx", "head"),
            P("head"),
        ),
        check_vma=False,
    )
```

```python
import functools

import jax
import jax.numpy as jnp
from jax import lax
from jax.experimental import pallas as pl
from jax.experimental.pallas import tpu as pltpu
from jax.sharding import PartitionSpec as P

DH = 128
HD = 8192


rate_unit = 2.0 ** (-20)
norm_eps = 1e-06
first_place = {"ctx": 36, "head": 14}
wide = jnp.float32
half = jnp.bfloat16


def swap(array, axis):
    size, first = lax.axis_size(axis), first_place[axis]
    groups = [[(first + slot) % size for slot in range(size)]]
    return lax.all_to_all(array, axis, 0, 0, axis_index_groups=groups)


def ctx_slots(members):
    return [(block - first_place["ctx"]) % members for block in range(members)]


def halves(array, axis):
    high = array.astype(half)
    low = (array - high.astype(wide)).astype(half)
    return jnp.concatenate([high, low], axis=axis)


def twice(array, axis):
    return jnp.concatenate([array, array], axis=axis)


def dot(left, right):
    return jnp.dot(left, right, preferred_element_type=wide)


def dot_nt(left, right):
    return lax.dot_general(left, right, (((1,), (1,)), ((), ())), preferred_element_type=wide)


def dot_tn(left, right):
    return lax.dot_general(left, right, (((0,), (0,)), ((), ())), preferred_element_type=wide)


def rate_of(ints_ref, head):
    return ints_ref[head].astype(wide) * rate_unit


def decay_column(rate, rows, late):
    place = lax.broadcasted_iota(jnp.int32, (rows, DH), 0).astype(wide)
    return jnp.exp(-rate * ((rows - 1.0 - place) if late else (place + 1.0)))


def decay_square(rate, rows):
    later = lax.broadcasted_iota(jnp.int32, (rows, rows), 0)
    sooner = lax.broadcasted_iota(jnp.int32, (rows, rows), 1)
    gap = (later - sooner).astype(wide)
    return jnp.where(gap >= 0.0, jnp.exp(-rate * jnp.maximum(gap, 0.0)), 0.0) * (1.0 / DH)


def cols(head):
    return slice(head * DH, (head + 1) * DH)


def summary_kernel(
    members, ints_ref, k_ref, v_ref, gain_ref, out_ref, spans_ref, gain_out_ref, ints, keys, values, late, arrived
):
    rows, features = k_ref.shape
    heads = features // DH
    copies = [
        pltpu.make_async_copy(source, target, arrived.at[number])
        for number, (source, target) in enumerate(
            ((ints_ref, ints), (k_ref, keys), (v_ref, values), (gain_ref, gain_out_ref))
        )
    ]
    for copy in copies:
        copy.start()
    copies[0].wait()
    slot = (lax.axis_index("ctx") + (members - first_place["ctx"])) % members
    owned = slot * (features // members) // DH
    power = lax.broadcasted_iota(jnp.int32, (8, DH), 0).astype(wide) + 1.0
    spans_ref[0:8, :] = jnp.exp(-(rate_of(ints, owned) * rows) * power)
    for head in range(heads):
        spans_ref[8 + head : 9 + head, :] = jnp.full((1, DH), rate_of(ints, head), wide)
        late[:, cols(head)] = decay_column(rate_of(ints, head), rows, True)
    copies[1].wait()
    copies[2].wait()
    for head in range(heads):
        weighted = late[:, cols(head)] * values[:, cols(head)].astype(wide)
        out_ref[cols(head), :] = dot(twice(keys[:, cols(head)].T, 1), halves(weighted, 0))
    copies[3].wait()


def scan_blocks(order, span, leap, take, put, zero):
    chains = [order[at : at + 8] for at in range(0, len(order), 8)]
    totals = [take(chain[0]) for chain in chains]
    for turn in range(1, 8):
        blocks = [take(chain[turn]) for chain in chains]
        totals = [span * total + block for total, block in zip(totals, blocks)]
    states = [zero]
    for total in totals[:-1]:
        states.append(leap * states[-1] + total)
    for turn in range(8):
        blocks = [take(chain[turn]) for chain in chains]
        for chain, state in zip(chains, states):
            put(chain[turn], state)
        states = [span * state + block for state, block in zip(states, blocks)]


def forward_kernel(members, spans_ref, in_ref, out_ref):
    chunk = in_ref.shape[0] // members

    def take(block):
        return in_ref[block * chunk : (block + 1) * chunk, :]

    def put(block, state):
        out_ref[block * chunk : (block + 1) * chunk, :] = state

    order = ctx_slots(members)
    scan_blocks(order, spans_ref[0:1, :], spans_ref[7:8, :], take, put, jnp.zeros((chunk, DH), wide))


def backward_kernel(members, spans_ref, in_ref, out_ref):
    step = in_ref.shape[0] // members
    chunk = step - 1

    def take(block):
        return in_ref[block * step : block * step + chunk, :]

    def put(block, state):
        out_ref[block * step : block * step + chunk, :] = state

    order = list(reversed(ctx_slots(members)))
    scan_blocks(order, spans_ref[0:1, :], spans_ref[7:8, :], take, put, jnp.zeros((chunk, DH), wide))
    gains = [in_ref[block * step + chunk : (block + 1) * step, :] for block in range(members)]
    while len(gains) > 1:
        gains = [gains[at] + gains[at + 1] for at in range(0, len(gains), 2)]
    for block in range(members):
        out_ref[block * step + chunk : (block + 1) * step, :] = gains[0]


def attend_kernel(
    spans_ref, q_ref, k_ref, v_ref, gate_ref, grad_ref, gain_ref, prefix_ref,
    attention_ref, stats_ref, weights_ref, gated_ref, scaled_ref, early_ref,
):
    rows, features = q_ref.shape
    squares = jnp.zeros((rows, DH), wide)
    crossed = jnp.zeros((rows, DH), wide)
    for head in range(features // DH):
        at = cols(head)
        rate = spans_ref[8 + head : 9 + head, :]
        queries = q_ref[:, at]
        weights = (dot_nt(queries, k_ref[:, at]) * decay_square(rate, rows)).astype(half)
        weights_ref[:, at] = weights
        gated = grad_ref[:, at].astype(wide) * jax.nn.sigmoid(gate_ref[:, at].astype(wide))
        gated_ref[:, at] = gated
        scaled = gated * gain_ref[:, at]
        scaled_ref[:, at] = scaled
        early = decay_column(rate, rows, False)
        early_ref[:, at] = early
        carried = dot(twice(queries, 1), halves(prefix_ref[at, :], 0)) * (1.0 / DH)
        attention = dot(weights, v_ref[:, at]) + early * carried
        attention_ref[:, at] = attention
        squares = squares + attention * attention
        crossed = crossed + scaled * attention
    squares = jnp.sum(squares.T, axis=0, keepdims=True)
    crossed = jnp.sum(crossed.T, axis=0, keepdims=True)
    pair = jnp.concatenate([squares, crossed], axis=0)
    for member in range(stats_ref.shape[0]):
        stats_ref[member] = pair


def token_scales(stats_ref):
    total = jnp.sum(stats_ref[...], axis=0)
    inverse = lax.rsqrt(total[0:1] * (1.0 / HD) + norm_eps)
    pull = inverse * inverse * inverse * total[1:2] * (1.0 / HD)
    line = lax.broadcasted_iota(jnp.int32, (8, DH), 0)
    columns = jnp.where(line == 0, inverse, jnp.where(line == 1, pull, 0.0)).T
    return columns[:, 0:1], columns[:, 1:2]


def ahead_kernel(
    members, stats_ref, attention_ref, gated_ref, scaled_ref, q_ref, early_ref, grad_ref, out_ref
):
    rows, features = attention_ref.shape
    heads = features // DH
    step = out_ref.shape[0] // members
    chunk = step - 1
    inverse, pull = token_scales(stats_ref)
    for head in range(heads):
        at = cols(head)
        attention = attention_ref[:, at]
        grad = (inverse * scaled_ref[:, at] - pull * attention).astype(half)
        grad_ref[:, at] = grad
        ahead = dot(twice(q_ref[:, at].T, 1), halves(early_ref[:, at] * grad.astype(wide), 0))
        for piece in range(DH // chunk):
            start = (head * (DH // chunk) + piece) * step
            out_ref[start : start + chunk, :] = ahead[piece * chunk : (piece + 1) * chunk, :]
        gain_row = jnp.sum(gated_ref[:, at] * (attention * inverse), axis=0, keepdims=True)
        for block in range(head, members, heads):
            out_ref[block * step + chunk : (block + 1) * step, :] = gain_row


def early_grads_kernel(
    spans_ref, stats_ref, attention_ref, scaled_ref, gate_ref, grad_ref, q_ref, k_ref, v_ref,
    weights_ref, prefix_ref, early_ref, grad_q_ref, grad_gate_ref, local_k_ref, local_v_ref, late_ref,
):
    rows, features = q_ref.shape
    inverse, _ = token_scales(stats_ref)
    for head in range(features // DH):
        at = cols(head)
        normed = attention_ref[:, at] * inverse
        rest = 1.0 - jax.nn.sigmoid(gate_ref[:, at].astype(wide))
        grad_gate_ref[:, at] = (scaled_ref[:, at] * normed * rest).astype(half)
        grad = grad_ref[:, at]
        rate = spans_ref[8 + head : 9 + head, :]
        late_ref[:, at] = decay_column(rate, rows, True) * (1.0 / DH)
        square = decay_square(rate, rows)
        grad_scores = (dot_nt(grad, v_ref[:, at]) * square).astype(half)
        carried = dot_nt(twice(grad, 1), halves(prefix_ref[at, :], 1)) * (1.0 / DH)
        grad_q = dot(grad_scores, k_ref[:, at]) + early_ref[:, at] * carried
        grad_q_ref[:, at] = grad_q.astype(half)
        local_k_ref[:, at] = dot_tn(grad_scores, q_ref[:, at])
        local_v_ref[:, at] = dot_tn(weights_ref[:, at], grad)


def final_kernel(
    members, back_ref, k_ref, v_ref, local_k_ref, local_v_ref, late_ref, grad_k_ref, grad_v_ref, gain_ref,
    keys, values, gain, left,
):
    rows, features = k_ref.shape
    heads = features // DH
    copies = []

    def send(source, target):
        copy = pltpu.make_async_copy(source, target, left.at[len(copies)])
        copy.start()
        copies.append(copy)

    step = back_ref.shape[0] // members
    chunk = step - 1
    pieces = DH // chunk
    for head in range(heads):
        gain[:, cols(head)] = back_ref[head * step + chunk : (head + 1) * step, :]
    send(gain, gain_ref)
    for head in range(heads):
        at = cols(head)
        late = late_ref[:, at]
        starts = [block * step for block in range(head * pieces, (head + 1) * pieces)]
        suffix = jnp.concatenate([back_ref[start : start + chunk, :] for start in starts], axis=0)
        high = suffix.astype(half)
        low = (suffix - high.astype(wide)).astype(half)
        carried_k = dot_nt(twice(v_ref[:, at], 1), jnp.concatenate([high, low], axis=1))
        carried_v = dot(twice(k_ref[:, at], 1), jnp.concatenate([high, low], axis=0))
        keys[:, at] = (local_k_ref[:, at] + late * carried_k).astype(half)
        values[:, at] = (local_v_ref[:, at] + late * carried_v).astype(half)
        if head % 2 == 1:
            both = slice((head - 1) * DH, (head + 1) * DH)
            send(keys.at[:, both], grad_k_ref.at[:, both])
            send(values.at[:, both], grad_v_ref.at[:, both])
    for copy in copies:
        copy.wait()


def call(kernel, name, shapes, *operands, place=pltpu.VMEM, out_place=pltpu.VMEM, scratch=(), flops=0, bytes_moved=0):
    out_shape = [jax.ShapeDtypeStruct(*shape) for shape in shapes]
    results = pl.pallas_call(
        kernel,
        out_shape=out_shape,
        in_specs=[pl.BlockSpec(memory_space=place)] * len(operands),
        out_specs=[pl.BlockSpec(memory_space=out_place)] * len(out_shape),
        scratch_shapes=list(scratch),
        compiler_params=pltpu.CompilerParams(vmem_limit_bytes=24 * 1024 * 1024),
        cost_estimate=pl.CostEstimate(flops=flops, bytes_accessed=bytes_moved, transcendentals=0),
        name=name,
    )(*operands)
    return results if len(out_shape) > 1 else results[0]


def body(queries, key_rows, value_rows, gate_in, grad_out, decay_ints, norm_gain):
    rows, features = queries.shape
    members = lax.axis_size("ctx")
    head_members = lax.axis_size("head")
    chunk = features // members
    step = chunk + 1
    area = rows * features
    flat = ((features, DH), wide)
    long = ((members * step, DH), wide)
    block_wide = ((rows, features), wide)
    block_half = ((rows, features), half)

    def across(array, width):
        shape = (members, width, DH) if width % 8 == 0 else (members, width, 1, DH)
        return swap(array.reshape(shape), "ctx").reshape(members * width, DH)

    def sized(kernel):
        return functools.partial(kernel, members)

    given = (decay_ints, key_rows, value_rows, norm_gain.reshape(1, features))
    summary, spans, gain = call(
        sized(summary_kernel),
        "summary",
        [flat, ((16, DH), wide), ((1, features), wide)],
        *[pltpu.with_memory_space_constraint(a, pltpu.HBM) for a in given],
        place=pltpu.HBM,
        scratch=[
            pltpu.SMEM(decay_ints.shape, jnp.int32),
            pltpu.VMEM((rows, features), half),
            pltpu.VMEM((rows, features), half),
            pltpu.VMEM((rows, features), wide),
            pltpu.SemaphoreType.DMA((4,)),
        ],
    )
    there = across(summary, chunk)
    prefix = across(call(sized(forward_kernel), "forward_scan", [flat], spans, there), chunk)
    attention, stats, weights, gated, scaled, early = call(
        attend_kernel,
        "attend",
        [block_wide, ((head_members, 2, rows), wide), block_half, block_wide, block_wide, block_wide],
        spans, queries, key_rows, value_rows, gate_in, grad_out, gain, prefix,
    )
    stats = swap(stats, "head")
    grad, message = call(
        sized(ahead_kernel),
        "ahead",
        [block_half, long],
        stats, attention, gated, scaled, queries, early,
    )
    there = across(message, step)
    grad_q, grad_gate, local_k, local_v, late = call(
        early_grads_kernel,
        "early_grads",
        [block_half, block_half, block_wide, block_wide, block_wide],
        spans, stats, attention, scaled, gate_in, grad, queries, key_rows, value_rows,
        weights, prefix, early,
        flops=20 * area * DH, bytes_moved=28 * area,
    )
    back = across(call(sized(backward_kernel), "backward_scan", [long], spans, there), step)
    grad_k, grad_v, grad_gain = call(
        sized(final_kernel),
        "final",
        [block_half, block_half, ((1, features), wide)],
        back, key_rows, value_rows, local_k, local_v, late,
        out_place=pltpu.HBM,
        scratch=[
            pltpu.VMEM((rows, features), half),
            pltpu.VMEM((rows, features), half),
            pltpu.VMEM((1, features), wide),
            pltpu.SemaphoreType.DMA((features // DH + 1,)),
        ],
    )
    return grad_q, grad_k, grad_v, grad_gate, grad_gain.reshape(features)


def solution(mesh):
    placed = (
        P("ctx", "head"),
        P("ctx", "head"),
        P("ctx", "head"),
        P("ctx", "head"),
        P("ctx", "head"),
        P("head"),
        P("head"),
    )
    return jax.shard_map(
        body,
        mesh=mesh,
        in_specs=placed,
        out_specs=(
            P("ctx", "head"),
            P("ctx", "head"),
            P("ctx", "head"),
            P("ctx", "head"),
            P("head"),
        ),
        check_vma=False,
    )
```
